256 devices in a mesh: dp: 2 (over core), fsdp: 32 (over z, x), col: 4 (over y).
Axes of the slice: x: 4, y: 4, z: 8, core: 2. Of those that a mesh axis runs over, the one named last changes fastest.
Arguments:
- acts: bfloat16 [12288, 12288], P(('dp', 'fsdp'), 'col'), may hold values from -6 to 6, as said below
- cotangent: bfloat16 [2, 12288, 1024], P(None, ('dp', 'fsdp'), 'col'), may hold values from -36 to 36, as said below
- base: bfloat16 [2, 12288, 1024], P(None, 'fsdp', 'col'), may hold values from -4 to 4, as said below
- adapter_a: bfloat16 [2, 12288, 32], replicated, may hold values from -0.5 to 0.5, as said below
- adapter_b: bfloat16 [2, 32, 1024], P(None, None, 'col'), may hold values from -6 to 6
- magnitude: float32 [2, 1024], P(None, 'col'), may hold values from 0.5 to 2
Outputs:
- grad_acts: bfloat16 [12288, 12288], P(('dp', 'fsdp'), 'col')
- grad_a: float32 [2, 12288, 32], replicated
- grad_b: float32 [2, 32, 1024], P(None, None, 'col')
- grad_mag: float32 [2, 1024], P(None, 'col')
The draws below stay inside these ranges and needn't reach their ends.
Inputs may be any that keep to these rules, and one draw needn't show every extreme that they name: `acts`: real-valued. `base`: real-valued. `cotangent`: real-valued. `adapter_a`: real-valued.
All inputs are finite; a program needn't handle non-finite values.
Results may differ from the reference program's by a relative error of at most 0.0075.
Values may be sent and summed in bfloat16 or wider, within the bound.
A program may use at most 128 MiB of HBM per device.

```python
import math
import jax
import jax.numpy as jnp
from jax import lax

D = 12288
KVD = 1024
R = 32
TOKENS = 12288


def shared_rows(key):
    return jax.random.truncated_normal(jax.random.fold_in(key, 97), -3.0, 3.0, (D,), jnp.float32)


def signed_factor(key, shape):
    key_sign, key_size = jax.random.split(key, 2)
    signs = jnp.where(jax.random.bernoulli(key_sign, 0.5, shape), 1.0, -1.0)
    return signs * jax.random.uniform(key_size, shape, jnp.float32, 0.6, 1.4)


def draw_acts(key, part):
    rows = shared_rows(key)
    key = jax.random.fold_in(key, 31)
    key_one, key_two = jax.random.split(key, 2)
    noise = jax.random.truncated_normal(key_one, -6.0, 6.0, (TOKENS, D), jnp.float32)
    weights = jax.random.truncated_normal(key_two, -3.0, 3.0, (TOKENS, 1), jnp.float32)
    share = 0.5
    mixed = math.sqrt(1.0 - share) * noise + math.sqrt(share) * weights * rows[None, :]
    return jnp.clip(mixed, -6.0, 6.0).astype(jnp.bfloat16)


def draw_adapter_a(key, part):
    rows = shared_rows(key)
    key = jax.random.fold_in(key, 41)
    key_one, key_two = jax.random.split(key, 2)
    noise = jax.random.truncated_normal(key_one, -6.0, 6.0, (2, D, R), jnp.float32)
    share = 0.5
    factors = signed_factor(key_two, (2, 1, R))
    mixed = math.sqrt(1.0 - share) * noise + math.sqrt(share) * rows[None, :, None] * factors
    return jnp.clip(mixed / math.sqrt(D), -0.5, 0.5).astype(jnp.bfloat16)


def draw_base(key, part):
    rows = shared_rows(key)
    key = jax.random.fold_in(key, 11)
    key_one, key_two, key_three, key_four = jax.random.split(key, 4)
    rising = 1.0 + 2.0 * jnp.arange(D, dtype=jnp.float32) / D
    entries = jax.random.truncated_normal(key_one, -6.0, 6.0, (2, D, KVD), jnp.float32)
    spread = math.log(10.0)
    share = 0.5
    factors = signed_factor(key_four, (2, 1, KVD))
    entries = math.sqrt(1.0 - share) * entries + math.sqrt(share) * rows[None, :, None] * factors
    row_scale = jnp.exp(jax.random.uniform(key_two, (2, D, 1), jnp.float32, 0.0, spread)) * rising[None, :, None]
    col_scale = jnp.exp(jax.random.uniform(key_three, (2, 1, KVD), jnp.float32, 0.0, spread))
    return jnp.clip(entries * row_scale * col_scale / (3.0 * math.sqrt(D)), -4.0, 4.0).astype(jnp.bfloat16)


def draw_cotangent(key, part):
    key = jax.random.fold_in(key, 23)
    key_one, key_two = jax.random.split(key, 2)
    rising = 1.0 + 2.0 * jnp.arange(TOKENS, dtype=jnp.float32) / TOKENS
    entries = jax.random.truncated_normal(key_one, -6.0, 6.0, (2, TOKENS, KVD), jnp.float32)
    spread = math.log(4.0)
    row_scale = jnp.exp(jax.random.uniform(key_two, (2, TOKENS, 1), jnp.float32, 0.0, spread)) * rising[None, :, None]
    return (entries * row_scale / 2.0).astype(jnp.bfloat16)


def block_scale(own_key, shape, cuts, least, largest):
    loudness, own = 1.0, jax.random.fold_in(own_key, 6)
    for axis_at, shards_of in cuts:
        draws = jnp.exp(jax.random.uniform(jax.random.fold_in(own, axis_at), (shards_of,), jnp.float32, least / len(cuts), largest / len(cuts)))
        loudness = loudness * jnp.repeat(draws, shape[axis_at] // shards_of).reshape([-1 if axis == axis_at else 1 for axis in range(len(shape))])
    return loudness


def scatter_about(own_key, shape, width, most, pieces=(), kind=jnp.bfloat16):
    result = jax.random.normal(own_key, shape, jnp.float32) * width
    if len(pieces) > 0:
        result = block_scale(own_key, shape, pieces, -0.22, 0.18) * result
    return jnp.clip(result, min=-most, max=most).astype(kind)


def setup_inputs(seed: int = 0) -> dict:
    splits = jax.random.split(jax.random.key(seed), 7)
    acts = draw_acts(jax.random.fold_in(splits[6], 71), 0)
    cotangent = draw_cotangent(jax.random.fold_in(splits[6], 71), 0)
    base = draw_base(jax.random.fold_in(splits[6], 71), 0)
    adapter_a = draw_adapter_a(jax.random.fold_in(splits[6], 71), 0)
    adapter_b = scatter_about(splits[4], (2, R, KVD), 1.0, 6.0, ((2, 4),))
    magnitude = jnp.clip(jnp.exp(math.log(2.0) - 1.3862944 * jax.random.uniform(splits[5], (2, KVD), jnp.float32) ** block_scale(splits[5], (2, KVD), ((1, 4),), -0.2, 0.2)), 0.5, 2.0)
    return dict(acts=acts, cotangent=cotangent, base=base, adapter_a=adapter_a, adapter_b=adapter_b, magnitude=magnitude)


def reference(acts, cotangent, base, adapter_a, adapter_b, magnitude):
    highest = lax.Precision.HIGHEST
    grad_input = jnp.zeros(acts.shape, jnp.float32)
    list_a = []
    list_b = []
    list_m = []
    for which in range(2):
        weight = base[which]
        down = adapter_a[which]
        upper = adapter_b[which]
        upper_wide = upper.astype(jnp.float32)
        cot_wide = cotangent[which].astype(jnp.float32)
        composed = weight.astype(jnp.float32) + jnp.dot(down, upper, preferred_element_type=jnp.float32)
        norms = jnp.sqrt(lax.optimization_barrier(jnp.sum(composed * composed, axis=0)))
        across = jnp.dot(down.astype(jnp.float32).T, composed, precision=highest)
        scaling = magnitude[which] / norms
        scaled = (cot_wide * scaling).astype(jnp.bfloat16)
        low_in = jnp.dot(acts, down, preferred_element_type=jnp.float32)
        low_out = jnp.dot(scaled, upper.T, preferred_element_type=jnp.float32).astype(jnp.bfloat16)
        base_out = jnp.dot(acts, weight, preferred_element_type=jnp.float32)
        full_out = base_out + jnp.dot(low_in, upper_wide, precision=highest)
        grad_mag = lax.optimization_barrier(jnp.sum(cot_wide * full_out, axis=0)) / norms
        token_b = jnp.dot(low_in.T, cot_wide, precision=highest)
        grad_b = scaling * (token_b - across * (grad_mag / norms))
        factor = scaling * grad_mag / norms
        grad_a = jnp.dot(acts.T, low_out, preferred_element_type=jnp.float32) - jnp.dot(composed * factor, upper_wide.T, precision=highest)
        grad_input = grad_input + jnp.dot(scaled, weight.T, preferred_element_type=jnp.float32)
        grad_input = grad_input + jnp.dot(low_out, down.T, preferred_element_type=jnp.float32)
        list_a.append(grad_a)
        list_b.append(grad_b)
        list_m.append(grad_mag)
    return (grad_input.astype(jnp.bfloat16), jnp.stack(list_a), jnp.stack(list_b), jnp.stack(list_m))
```

```python
import functools

import jax
import jax.numpy as jnp
from jax import lax
from jax.experimental import pallas as pl
from jax.experimental.pallas import tpu as pltpu
from jax.sharding import PartitionSpec as P

MESH = pl.DeviceIdType.MESH
F32 = jnp.float32
BF16 = jnp.bfloat16

NX, NZ, NY = 4, 8, 4
NQ = 2 * NY

TOK = 192
TOK2 = 2 * TOK
FEAT = 3072
HALF = FEAT // 2
COLS = 256
ROWS = 384
RANK = 32
CUT = 192

NT = (((1,), (1,)), ((), ()))
TN = (((0,), (0,)), ((), ()))
NN = (((1,), (0,)), ((), ()))


def dot(a, b, dims=NN):
    return lax.dot_general(a, b, dims, preferred_element_type=F32)


def pieces(value, count):
    out = []
    for _ in range(count):
        part = value.astype(BF16)
        out.append(part)
        value = value - part.astype(F32)
    return out


def total(ref, count):
    value = ref[0]
    for i in range(1, count):
        value = value + ref[i]
    return value


def kernel(
    acts, cot, base, at, b, mag,
    gx_out, ga_out, gb_out, gm_out,
    w, actsf, gf, scaled, bf, ah,
    sqx, sqz, ns, tbp, tbi, ctp, cti, ctx, ctz, ctc,
    tpp, tpi, tps, tpzi, tpg, tpf, mox, moz, moq, gaf, gxb, lowo, momt,
    ssem, rsem,
):
    p = lax.axis_index("dp")
    f = lax.axis_index("fsdp")
    y = lax.axis_index("col")
    x = lax.rem(f, NX)
    z = lax.div(f, NX)
    q = 2 * y + p

    def at_xz(nx, nz):
        return (p, nz * NX + nx, y)

    def at_q(nq):
        return (lax.rem(nq, 2), f, lax.div(nq, 2))

    xpeer = lambda d: at_xz(lax.rem(x + d, NX), z)
    zpeer = lambda d: at_xz(x, lax.rem(z + d, NZ))
    qpeer = lambda d: at_q(lax.rem(q + d, NQ))
    ypeer = lambda d: (p, f, lax.rem(y + d, NY))
    core = (1 - p, f, y)
    swap = (lax.rem(z, 2), q * NX + x, lax.div(z, 2))
    fixed = z == q

    n_sem = [0]
    finals = []

    def sems(n):
        n_sem[0] += n
        assert n_sem[0] <= SEMS
        return n_sem[0] - n

    def copy(src, dst, sem, dev):
        return pltpu.make_async_remote_copy(
            src_ref=src, dst_ref=dst, send_sem=ssem.at[sem], recv_sem=rsem.at[sem],
            device_id=dev, device_id_type=MESH,
        )

    def each(lo, hi, body):
        def step(i, carry):
            body(i)
            return carry

        lax.fori_loop(lo, hi, step, 0)

    class Ring:
        def __init__(self, n, me, peer, dst):
            self.n, self.me, self.peer, self.dst = n, me, peer, dst
            self.sem = sems(n)

        def start(self, src):
            def mk(d):
                return copy(src(lax.rem(self.me + d, self.n)), self.dst.at[self.me], self.sem + d, self.peer(d))

            each(1, self.n, lambda d: mk(d).start())
            finals.append(lambda: each(1, self.n, lambda d: mk(d).wait_send()))

        def wait(self):
            def one(d):
                here = self.dst.at[lax.rem(self.me - d + self.n, self.n)]
                copy(here, here, self.sem + d, self.peer(d)).wait_recv()

            each(1, self.n, one)

    bar = pltpu.get_barrier_semaphore()
    each(1, NX, lambda d: pl.semaphore_signal(bar, inc=1, device_id=xpeer(d), device_id_type=MESH))
    each(1, NZ, lambda d: pl.semaphore_signal(bar, inc=1, device_id=zpeer(d), device_id_type=MESH))
    each(1, NQ, lambda d: pl.semaphore_signal(bar, inc=1, device_id=qpeer(d), device_id_type=MESH))

    @pl.when(jnp.logical_not(fixed))
    def _():
        pl.semaphore_signal(bar, inc=1, device_id=swap, device_id_type=MESH)
        pl.semaphore_wait(bar, NX + NZ + NQ - 2)

    @pl.when(fixed)
    def _():
        pl.semaphore_wait(bar, NX + NZ + NQ - 3)

    PARTS = ((0, CUT), (CUT, ROWS))
    s_swap = sems(2)

    def swap_copy(i):
        lo, hi = PARTS[i]
        return copy(base.at[p, pl.ds(lo, hi - lo), :], w.at[q, x, pl.ds(lo, hi - lo), :], s_swap + i, swap)

    @pl.when(jnp.logical_not(fixed))
    def _():
        swap_copy(1).start()
        swap_copy(0).start()

    def wait_swap(i):
        lo, hi = PARTS[i]
        here = w.at[z, x, pl.ds(lo, hi - lo), :]

        @pl.when(jnp.logical_not(fixed))
        def _():
            copy(here, here, s_swap + i, swap).wait_recv()

        @pl.when(fixed)
        def _():
            w[z, x, lo:hi, :] = base[p, lo:hi, :]

    def final_swap():
        @pl.when(jnp.logical_not(fixed))
        def _():
            swap_copy(0).wait_send()
            swap_copy(1).wait_send()

    finals.append(final_swap)

    s_acts = sems(1)
    mine = pl.ds(pl.multiple_of(p * TOK, TOK), TOK)
    others = pl.ds(pl.multiple_of((1 - p) * TOK, TOK), TOK)
    my_half = pl.ds(pl.multiple_of(p * HALF, HALF), HALF)
    other_half = pl.ds(pl.multiple_of((1 - p) * HALF, HALF), HALF)
    acts_copy = copy(acts.at[:, other_half], actsf.at[mine, :], s_acts, core)
    acts_copy.start()
    finals.append(acts_copy.wait_send)

    s_goty, s_gotc = sems(2 * NY), sems(2 * NY)

    def cot_y(d, k):
        return copy(cot.at[k], gf.at[2 * y + k, mine, :], s_goty + 2 * d + k, ypeer(d))

    def cot_c(d, k, src=None):
        there = gf.at[2 * lax.rem(y - d + NY, NY) + k, mine, :]
        return copy(there if src is None else src, there, s_gotc + 2 * d + k, core)

    def cot_start(d):
        for k in range(2):
            cot_y(d, k).start()

    each(1, NY, cot_start)
    for k in range(2):
        cot_c(0, k, cot.at[k]).start()
    finals.append(lambda: [cot_c(0, k, cot.at[k]).wait_send() for k in range(2)])

    def cot_final(d):
        for k in range(2):
            cot_y(d, k).wait_send()
            cot_c(d, k).wait_send()

    finals.append(lambda: each(1, NY, cot_final))

    def cot_relay():
        def one(d):
            for k in range(2):
                here = gf.at[2 * lax.rem(y - d + NY, NY) + k, mine, :]
                copy(here, here, s_goty + 2 * d + k, core).wait_recv()
                cot_c(d, k).start()

        each(1, NY, one)

    def cot_wait():
        def one(d):
            for k in range(2):
                here = gf.at[2 * lax.rem(y - d + NY, NY) + k, others, :]
                copy(here, here, s_gotc + 2 * d + k, core).wait_recv()

        each(0, NY, one)

    r_b = Ring(NY, y, ypeer, bf)
    r_b.start(lambda _: b)
    bf[y] = b[...]

    s_ax, s_az, s_bz, s_bx = sems(NX), sems(NX * 8), sems(8), sems(9 * NX)

    def ring_rows(part, way, s):
        lo, hi = PARTS[part]
        if s < 3:
            return lo, hi - lo
        half = (hi - lo) // 2
        return lo + way * half, half

    def origin(way, s):
        return lax.rem(z - s + NZ, NZ) if way == 0 else lax.rem(z + s, NZ)

    def z_copy(part, j, way, s):
        lo, n = ring_rows(part, way, s)
        here = w.at[origin(way, s), lax.rem(x - j + NX, NX), pl.ds(lo, n), :]
        sem = (s_az + (j * 2 + way) * 4 + s) if part == 0 else (s_bz + way * 4 + s)
        return copy(here, here, sem, zpeer(1 if way == 0 else NZ - 1))

    def z_arrival(part, j, way, s):
        lo, n = ring_rows(part, way, s)
        here = w.at[origin(way, s + 1), lax.rem(x - j + NX, NX), pl.ds(lo, n), :]
        sem = (s_az + (j * 2 + way) * 4 + s) if part == 0 else (s_bz + way * 4 + s)
        copy(here, here, sem, zpeer(1)).wait_recv()

    def z_start(part, j, way, s):
        z_copy(part, j, way, s).start()
        finals.append(lambda: z_copy(part, j, way, s).wait_send())

    def bx_copy(d, way, s):
        lo, n = ring_rows(1, way, s - 1)
        here = w.at[origin(way, s), x, pl.ds(lo, n), :]
        slot = 0 if s == 0 else 1 + way * 4 + s - 1
        return copy(here, here, s_bx + slot * NX + d, xpeer(d))

    def bx_start(way, s):
        each(1, NX, lambda d: bx_copy(d, way, s).start())
        finals.append(lambda: each(1, NX, lambda d: bx_copy(d, way, s).wait_send()))

    def bx_wait(way, s):
        lo, n = ring_rows(1, way, s - 1)
        slot = 0 if s == 0 else 1 + way * 4 + s - 1

        def one(d):
            here = w.at[origin(way, s), lax.rem(x - d + NX, NX), pl.ds(lo, n), :]
            copy(here, here, s_bx + slot * NX + d, xpeer(d)).wait_recv()

        each(1, NX, one)

    def ax_copy(d):
        here = w.at[z, x, pl.ds(0, CUT), :]
        return copy(here, here, s_ax + d, xpeer(d))

    def ax_wait(d):
        here = w.at[z, lax.rem(x - d + NX, NX), pl.ds(0, CUT), :]
        copy(here, here, s_ax + d, xpeer(d)).wait_recv()

    r_sqx = Ring(NX, x, xpeer, sqx)
    r_sqz = Ring(NZ, z, zpeer, sqz)
    r_ns = Ring(NQ, q, qpeer, ns)
    a_rows = at[p, :, pl.ds(pl.multiple_of(f * ROWS, ROWS), ROWS)]
    composed = base[p].astype(F32) + dot(a_rows, b[p], TN)
    sqx[x] = jnp.broadcast_to(jnp.sum(composed * composed, axis=0, keepdims=True), (8, COLS))
    r_sqx.start(lambda _: sqx.at[x])
    across = functools.reduce(lambda u, v: u + v, [dot(a_rows, c) for c in pieces(composed, 3)])

    wait_swap(1)
    for way in range(2):
        z_start(1, 0, way, 0)
    wait_swap(0)
    each(1, NX, lambda d: ax_copy(d).start())
    finals.append(lambda: each(1, NX, lambda d: ax_copy(d).wait_send()))
    for way in range(2):
        z_start(0, 0, way, 0)
    bx_start(0, 0)

    ah[0:RANK] = at[0, :, pl.ds(pl.multiple_of(q * HALF, HALF), HALF)]
    ah[RANK:] = at[1, :, pl.ds(pl.multiple_of(q * HALF, HALF), HALF)]
    actsf[mine, :] = acts[:, my_half]
    for k in range(2):
        gf[2 * y + k, mine, :] = cot[k]

    r_sqx.wait()
    sqz[z] = total(sqx, NX)
    r_sqz.start(lambda _: sqz.at[z])

    for j in range(1, NX):
        ax_wait(j)
        for way in range(2):
            z_start(0, j, way, 0)

    here_acts = actsf.at[others, :]
    copy(here_acts, here_acts, s_acts, core).wait_recv()
    low_in = dot(ah[...], actsf[...], NT)

    r_sqz.wait()
    norms = jnp.sqrt(total(sqz, NZ)[0:1])
    ns[q, 0:1] = norms
    ns[q, 1:2] = mag[pl.ds(p, 1), :] / norms
    r_ns.start(lambda _: ns.at[q])
    cot_relay()

    def ring_b(s):
        for way in range(2):
            z_arrival(1, 0, way, s - 1)
            if s < 4:
                z_start(1, 0, way, s)
            bx_start(way, s)

    def ring_a(s):
        for j in range(NX):
            for way in range(2):
                z_arrival(0, j, way, s - 1)
                if s < 4:
                    z_start(0, j, way, s)

    def forward(zi):
        out = dot(actsf[...], w[zi].reshape(NX * ROWS, COLS))
        momt[pl.ds(zi, 1), :] = jnp.sum(out * gf[zi].astype(F32), axis=0, keepdims=True)

    ring_b(1)
    r_b.wait()
    cot_wait()

    r_tb = Ring(NQ, q, qpeer, tbi)
    for k in range(2):
        parts = jnp.concatenate(pieces(low_in[k * RANK : (k + 1) * RANK], 3), axis=0)
        for yy in range(NY):
            t = dot(parts, gf[2 * yy + k])
            tbp[2 * yy + k] = t[0:RANK] + t[RANK : 2 * RANK] + t[2 * RANK :]
    tbi[q] = tbp[q]
    r_tb.start(lambda i: tbp.at[i])

    ring_a(1)

    r_ns.wait()
    low = []
    for k in range(2):
        acc = None
        for yy in range(NY):
            i = 2 * yy + k
            s = (gf[i].astype(F32) * ns[i, 1:2]).astype(BF16)
            scaled[i] = s
            t = dot(s, bf[yy, k], NT)
            acc = t if acc is None else acc + t
        low.append(acc)
    lowf = jnp.concatenate(low, axis=1)
    lowo[...] = lowf.astype(BF16)
    lowt = lowf.T.astype(BF16)
    r_tpx = Ring(NX, x, xpeer, tpi)
    for xx in range(NX):
        tpp[xx] = dot(lowt, actsf[:, xx * ROWS : (xx + 1) * ROWS])
    tpi[x] = tpp[x]
    r_tpx.start(lambda i: tpp.at[i])

    ring_b(2)

    bx_wait(0, 0)
    forward(z)
    for way in range(2):
        bx_wait(way, 1)
        forward(origin(way, 1))

    r_tb.wait()
    token_b = total(tbi, NQ)
    r_ctz = Ring(NZ, z, zpeer, cti)
    r_ctx = Ring(NX, x, xpeer, ctx)
    r_ctg = Ring(NZ, z, zpeer, ctz)
    for g in range(NZ):
        ctp[g, 0:4] = across[4 * g : 4 * g + 4]
        ctp[g, 4:8] = token_b[4 * g : 4 * g + 4]
    cti[z] = ctp[z]
    r_ctz.start(lambda i: ctp.at[i])

    ring_a(2)

    r_tpz = Ring(NZ, z, zpeer, tpzi)
    r_tpg = Ring(NZ, z, zpeer, tpg)
    r_tpf = Ring(NX, x, xpeer, tpf)
    r_tpx.wait()
    tps[...] = total(tpi, NX).reshape(NZ, 8, ROWS)
    tpzi[z] = tps[z]
    r_tpz.start(lambda i: tps.at[i])

    ring_b(3)

    for way in range(2):
        bx_wait(way, 2)
        forward(origin(way, 2))

    r_ctz.wait()
    ctx[x] = total(cti, NZ)
    r_ctx.start(lambda _: ctx.at[x])
    r_tpz.wait()
    tpg[z] = total(tpzi, NZ)
    r_tpg.start(lambda _: tpg.at[z])

    ring_a(3)

    r_ctx.wait()
    ctz[z] = total(ctx, NX)
    r_ctg.start(lambda _: ctz.at[z])
    r_tpg.wait()
    tpf[x] = tpg[...]
    r_tpf.start(lambda _: tpg)

    ring_b(4)

    for way in range(2):
        bx_wait(way, 3)
        forward(origin(way, 3))

    r_ctg.wait()
    ctc[p] = ctz[...]
    s_ctc = sems(1)
    ctc_copy = copy(ctz, ctc.at[p], s_ctc, core)
    ctc_copy.start()
    finals.append(ctc_copy.wait_send)

    ring_a(4)

    for way in range(2):
        bx_wait(way, 4)
    forward(origin(0, 4))

    r_mox = Ring(NX, x, xpeer, mox)
    r_moz = Ring(NZ, z, zpeer, moz)
    r_moq = Ring(NQ, q, qpeer, moq)
    extra = []
    for i in range(NQ):
        extra.append(jnp.sum(tbp[i] * bf[i // 2, i % 2].astype(F32), axis=0, keepdims=True))
    mox[x] = momt[...] + jnp.concatenate(extra, axis=0)
    r_mox.start(lambda _: mox.at[x])

    def backward(xx):
        acc = dot(lowo[...], ah[:, xx * ROWS : (xx + 1) * ROWS])
        for zi in range(NZ):
            acc = acc + dot(scaled[zi], w[zi, xx], NT)
        gxb[:, xx * ROWS : (xx + 1) * ROWS] = acc.astype(BF16)

    backward(0)
    r_mox.wait()
    moz[z] = total(mox, NX)
    r_moz.start(lambda _: moz.at[z])
    backward(1)
    backward(2)
    r_moz.wait()
    moq[q] = total(moz, NZ)
    r_moq.start(lambda _: moq.at[q])
    backward(3)

    s_gx = sems(1)
    gx_copy = copy(gxb.at[others, :], gx_out.at[:, my_half], s_gx, core)
    gx_copy.start()
    finals.append(gx_copy.wait_send)
    gx_out[:, my_half] = gxb[mine, :]

    r_moq.wait()
    moment = total(moq, NQ)
    norm_all = jnp.concatenate([ns[i, 0:1] for i in range(NQ)], axis=0)
    scal_all = jnp.concatenate([ns[i, 1:2] for i in range(NQ)], axis=0)
    grad_mag = moment / norm_all
    factor = scal_all * grad_mag / norm_all
    momt[...] = grad_mag

    r_tpf.wait()
    for k in range(2):
        weights = []
        inner = None
        for yy in range(NY):
            i = 2 * yy + k
            two = jnp.concatenate(pieces(bf[yy, k].astype(F32) * factor[i : i + 1], 2), axis=0)
            weights.append(two)
            t = dot(two, bf[yy, k], NT)
            inner = t if inner is None else inner + t
        inner = jnp.concatenate(pieces(inner[0:RANK] + inner[RANK:], 2), axis=0)
        for xx in range(NX):
            span = slice(xx * ROWS, (xx + 1) * ROWS)
            acc = dot(inner, ah[k * RANK : (k + 1) * RANK, span])
            for yy in range(NY):
                acc = acc + dot(weights[yy], w[2 * yy + k, xx], NT)
            tokens = tpf[xx].reshape(2 * RANK, ROWS)[k * RANK : (k + 1) * RANK]
            gaf[q, k * RANK : (k + 1) * RANK, span] = (tokens - (acc[0:RANK] + acc[RANK:])).astype(BF16)

    s_gay, s_gac = sems(NY), sems(NY)

    def ga_y(d):
        return copy(gaf.at[q], gaf.at[q], s_gay + d, ypeer(d))

    def ga_c(d):
        here = gaf.at[2 * lax.rem(y - d + NY, NY) + p]
        return copy(here, here, s_gac + d, core)

    each(1, NY, lambda d: ga_y(d).start())
    ga_c(0).start()

    copy(ctc.at[1 - p], ctc.at[1 - p], s_ctc, core).wait_recv()
    for k in range(2):
        i = 2 * y + k
        norm_k = ns[i, 0:1]
        scal_k = ns[i, 1:2]
        gm_k = momt[pl.ds(i, 1), :]
        gm_out[k : k + 1] = gm_k
        ratio = gm_k / norm_k
        for g in range(NZ):
            gb_out[k, 4 * g : 4 * g + 4] = scal_k * (ctc[k, g, 4:8] - ctc[k, g, 0:4] * ratio)

    def ga_relay(d):
        here = gaf.at[2 * lax.rem(y - d + NY, NY) + p]
        copy(here, here, s_gay + d, core).wait_recv()
        ga_c(d).start()

    each(1, NY, ga_relay)

    def ga_wait(d):
        here = gaf.at[2 * lax.rem(y - d + NY, NY) + 1 - p]
        copy(here, here, s_gac + d, core).wait_recv()

    each(0, NY, ga_wait)
    for i in range(NQ):
        for k in range(2):
            ga_out[k, :, i * HALF : (i + 1) * HALF] = gaf[i, k * RANK : (k + 1) * RANK]

    def ga_final(d):
        ga_y(d).wait_send()
        ga_c(d).wait_send()

    each(1, NY, ga_final)
    ga_c(0).wait_send()
    here_gx = gx_out.at[:, other_half]
    copy(here_gx, here_gx, s_gx, core).wait_recv()
    for final in finals:
        final()


SEMS = 256


def on_device(acts, cot, base, adapter_a, adapter_b, magnitude):
    at = jnp.swapaxes(adapter_a, 1, 2)
    vm = pl.BlockSpec(memory_space=pltpu.VMEM)
    scratch = [
        ((NZ, NX, ROWS, COLS), BF16),
        ((TOK2, HALF), BF16),
        ((NQ, TOK2, COLS), BF16),
        ((NQ, TOK2, COLS), BF16),
        ((NY, 2, RANK, COLS), BF16),
        ((2 * RANK, HALF), BF16),
        ((NX, 8, COLS), F32),
        ((NZ, 8, COLS), F32),
        ((NQ, 8, COLS), F32),
        ((NQ, RANK, COLS), F32),
        ((NQ, RANK, COLS), F32),
        ((NZ, 8, COLS), F32),
        ((NZ, 8, COLS), F32),
        ((NX, 8, COLS), F32),
        ((NZ, 8, COLS), F32),
        ((2, NZ, 8, COLS), F32),
        ((NX, 2 * RANK, ROWS), F32),
        ((NX, 2 * RANK, ROWS), F32),
        ((NZ, 8, ROWS), F32),
        ((NZ, 8, ROWS), F32),
        ((NZ, 8, ROWS), F32),
        ((NX, NZ, 8, ROWS), F32),
        ((NX, 8, COLS), F32),
        ((NZ, 8, COLS), F32),
        ((NQ, 8, COLS), F32),
        ((NQ, 2 * RANK, HALF), BF16),
        ((TOK2, HALF), BF16),
        ((TOK2, 2 * RANK), BF16),
        ((NQ, COLS), F32),
    ]
    gx, ga, gb, gm = pl.pallas_call(
        kernel,
        out_shape=(
            jax.ShapeDtypeStruct((TOK, FEAT), BF16),
            jax.ShapeDtypeStruct((2, RANK, NQ * HALF), BF16),
            jax.ShapeDtypeStruct((2, RANK, COLS), F32),
            jax.ShapeDtypeStruct((2, COLS), F32),
        ),
        in_specs=[vm] * 6,
        out_specs=(vm,) * 4,
        scratch_shapes=[pltpu.VMEM(shape, dtype) for shape, dtype in scratch]
        + [pltpu.SemaphoreType.DMA((SEMS,)), pltpu.SemaphoreType.DMA((SEMS,))],
        compiler_params=pltpu.CompilerParams(
            collective_id=0, has_side_effects=True, vmem_limit_bytes=56 * 2**20
        ),
        cost_estimate=pl.CostEstimate(flops=5 * 10**9, bytes_accessed=8 * 10**6, transcendentals=0),
    )(acts, cot, base, at, adapter_b, magnitude)
    return gx, jnp.swapaxes(ga.astype(F32), 1, 2), gb, gm


def solution(mesh):
    in_specs = (
        P(("dp", "fsdp"), "col"),
        P(None, ("dp", "fsdp"), "col"),
        P(None, "fsdp", "col"),
        P(),
        P(None, None, "col"),
        P(None, "col"),
    )
    out_specs = (P(("dp", "fsdp"), "col"), P(), P(None, None, "col"), P(None, "col"))
    return jax.shard_map(
        on_device, mesh=mesh, in_specs=in_specs, out_specs=out_specs, check_vma=False
    )
```

```python
import functools

import jax
import jax.numpy as jnp
from jax import lax
from jax.experimental import pallas as pl
from jax.experimental.pallas import tpu as pltpu
from jax.sharding import PartitionSpec as P

MESH = pl.DeviceIdType.MESH
F32 = jnp.float32
BF16 = jnp.bfloat16

NX, NZ, NY = 4, 8, 4
NQ = 2 * NY

TOK = 192
TOK2 = 2 * TOK
FEAT = 3072
HALF = FEAT // 2
COLS = 256
ROWS = 384
RANK = 32
CUT = 160

NT = (((1,), (1,)), ((), ()))
TN = (((0,), (0,)), ((), ()))
NN = (((1,), (0,)), ((), ()))


def dot(a, b, dims=NN):
    return lax.dot_general(a, b, dims, preferred_element_type=F32)


def pieces(value, count):
    out = []
    for _ in range(count):
        part = value.astype(BF16)
        out.append(part)
        value = value - part.astype(F32)
    return out


def total(ref, count):
    value = ref[0]
    for i in range(1, count):
        value = value + ref[i]
    return value


def kernel(
    acts, cot, base, at, b, mag,
    gx_out, ga_out, gb_out, gm_out,
    w, actsf, gf, scaled, bf, ah, ar, mybase,
    sqx, sqz, ns, tbp, tbi, ctp, cti, ctx, ctz, ctc,
    tpp, tpi, tps, tpzi, tpg, mox, moz, moq, gaf, gxb, lowo, momt, wts, inr,
    ssem, rsem, lsem,
):
    p = lax.axis_index("dp")
    f = lax.axis_index("fsdp")
    y = lax.axis_index("col")
    x = lax.rem(f, NX)
    z = lax.div(f, NX)
    q = 2 * y + p

    def at_xz(nx, nz):
        return (p, nz * NX + nx, y)

    def at_q(nq):
        return (lax.rem(nq, 2), f, lax.div(nq, 2))

    xpeer = lambda d: at_xz(lax.rem(x + d, NX), z)
    zpeer = lambda d: at_xz(x, lax.rem(z + d, NZ))
    qpeer = lambda d: at_q(lax.rem(q + d, NQ))
    ypeer = lambda d: (p, f, lax.rem(y + d, NY))
    core = (1 - p, f, y)

    def shift(c):
        k, half = lax.rem(c, 2), lax.div(c, 2)
        return lax.rem((1 - k) * half + k * (4 + (4 - half) * jnp.minimum(half, 1)), NZ)

    def chunk_at(position):
        step = lax.rem(position - q + NZ, NZ)
        far = lax.div(step, 4)
        return (1 - far) * 2 * step + far * lax.rem(17 - 2 * step, NZ)

    target = (lax.rem(z, 2), lax.rem(z + shift(q), NZ) * NX + x, lax.div(z, 2))
    own = chunk_at(z)
    source = (lax.rem(own, 2), q * NX + x, lax.div(own, 2))
    fixed = jnp.logical_and(own == q, z == q)

    counts = {"send": 0, "recv": 0, "local": 0}
    limits = {"send": SENDS, "recv": RECVS, "local": LOCALS}
    finals = []

    def sems(kind, n=1):
        counts[kind] += n
        assert counts[kind] <= limits[kind]
        return counts[kind] - n

    def copy(src, dst, send, recv, dev):
        return pltpu.make_async_remote_copy(
            src_ref=src, dst_ref=dst, send_sem=ssem.at[send], recv_sem=rsem.at[recv],
            device_id=dev, device_id_type=MESH,
        )

    def arrived(ref, recv):
        copy(ref, ref, 0, recv, core).wait_recv()

    def sent(ref, send):
        finals.append(lambda: copy(ref, ref, send, 0, core).wait_send())

    def each(lo, hi, body):
        def step(i, carry):
            body(i)
            return carry

        lax.fori_loop(lo, hi, step, 0)

    class Ring:
        def __init__(self, n, me, peer, dst):
            self.n, self.me, self.peer, self.dst = n, me, peer, dst
            self.send, self.recv = sems("send"), sems("recv")

        def start(self, src):
            def one(d):
                block = src(lax.rem(self.me + d, self.n))
                copy(block, self.dst.at[self.me], self.send, self.recv, self.peer(d)).start()

            each(1, self.n, one)
            sent(self.dst.at[pl.ds(0, self.n - 1)], self.send)

        def wait(self):
            arrived(self.dst.at[pl.ds(0, self.n - 1)], self.recv)

    mine = pl.ds(pl.multiple_of(p * TOK, TOK), TOK)
    others = pl.ds(pl.multiple_of((1 - p) * TOK, TOK), TOK)
    my_half = pl.ds(pl.multiple_of(p * HALF, HALF), HALF)
    other_half = pl.ds(pl.multiple_of((1 - p) * HALF, HALF), HALF)

    loads = [
        pltpu.make_async_copy(base.at[p], mybase, lsem.at[sems("local")]),
        pltpu.make_async_copy(at.at[p, :, pl.ds(pl.multiple_of(f * ROWS, ROWS), ROWS)], ar, lsem.at[sems("local")]),
    ]
    for k in range(2):
        rows = pl.ds(k * RANK, RANK)
        span = pl.ds(pl.multiple_of(q * HALF, HALF), HALF)
        loads.append(pltpu.make_async_copy(at.at[k, :, span], ah.at[rows, :], lsem.at[sems("local")]))
        loads.append(pltpu.make_async_copy(cot.at[k], gf.at[2 * y + k, mine, :], lsem.at[sems("local")]))
    loads.append(pltpu.make_async_copy(acts.at[:, my_half], actsf.at[mine, :], lsem.at[sems("local")]))
    for load in loads:
        load.start()

    bar = pltpu.get_barrier_semaphore()
    each(1, NX, lambda d: pl.semaphore_signal(bar, inc=1, device_id=xpeer(d), device_id_type=MESH))
    each(1, NZ, lambda d: pl.semaphore_signal(bar, inc=1, device_id=zpeer(d), device_id_type=MESH))
    each(1, NQ, lambda d: pl.semaphore_signal(bar, inc=1, device_id=qpeer(d), device_id_type=MESH))

    @pl.when(jnp.logical_not(fixed))
    def _():
        pl.semaphore_signal(bar, inc=1, device_id=source, device_id_type=MESH)

    r_sqx = Ring(NX, x, xpeer, sqx)
    r_sqz = Ring(NZ, z, zpeer, sqz)
    r_ns = Ring(NQ, q, qpeer, ns)
    bf[y] = b[...]
    for load in loads:
        load.wait()
    composed = mybase[...].astype(F32) + dot(ar[...], b[p], TN)
    sqx[x] = jnp.broadcast_to(jnp.sum(composed * composed, axis=0, keepdims=True), (8, COLS))
    across = functools.reduce(lambda u, v: u + v, [dot(ar[...], c) for c in pieces(composed, 3)])

    @pl.when(jnp.logical_not(fixed))
    def _():
        pl.semaphore_wait(bar, NX + NZ + NQ - 2)

    @pl.when(fixed)
    def _():
        pl.semaphore_wait(bar, NX + NZ + NQ - 3)

    PARTS = ((0, CUT), (CUT, ROWS))
    s_swap, r_swap = sems("send"), sems("recv", 2)

    def swap_copy(i):
        lo, hi = PARTS[i]
        return copy(mybase.at[pl.ds(lo, hi - lo), :], w.at[q, x, pl.ds(lo, hi - lo), :], s_swap, r_swap + i, target)

    @pl.when(jnp.logical_not(fixed))
    def _():
        swap_copy(1).start()
        swap_copy(0).start()

    def wait_swap(i):
        lo, hi = PARTS[i]

        @pl.when(jnp.logical_not(fixed))
        def _():
            arrived(w.at[own, x, pl.ds(lo, hi - lo), :], r_swap + i)

        @pl.when(fixed)
        def _():
            w[own, x, lo:hi, :] = mybase[lo:hi, :]

    def final_swap():
        @pl.when(jnp.logical_not(fixed))
        def _():
            copy(mybase, mybase, s_swap, 0, target).wait_send()

    finals.append(final_swap)
    r_sqx.start(lambda _: sqx.at[x])

    s_acts, r_acts = sems("send"), sems("recv")
    copy(acts.at[:, other_half], actsf.at[mine, :], s_acts, r_acts, core).start()
    sent(actsf.at[mine, :], s_acts)

    s_goty, s_gotc, r_goty, r_gotc = sems("send"), sems("send"), sems("recv", NY), sems("recv")

    def cot_core(d):
        for k in range(2):
            here = gf.at[2 * lax.rem(y - d + NY, NY) + k, mine, :]
            copy(here, here, s_gotc, r_gotc, core).start()

    def cot_start():
        def one(d):
            for k in range(2):
                here = gf.at[2 * y + k, mine, :]
                copy(here, here, s_goty, r_goty + d, ypeer(d)).start()

        each(1, NY, one)
        cot_core(0)
        sent(gf.at[pl.ds(0, NY - 1)], s_goty)
        sent(gf.at[pl.ds(0, NY)], s_gotc)

    def cot_relay():
        def one(d):
            arrived(gf.at[0], r_goty + d)
            cot_core(d)

        each(1, NY, one)

    def cot_wait():
        arrived(gf.at[pl.ds(0, NY)], r_gotc)

    r_b = Ring(NY, y, ypeer, bf)
    r_b.start(lambda i: bf.at[y])

    s_ax, s_az, s_bz, s_bx = sems("send"), sems("send"), sems("send"), sems("send")
    r_ax, r_az, r_bz = sems("recv", NX), sems("recv", NX * 8), sems("recv", 8)
    r_bx, r_bx4 = sems("recv", 7 * 3), sems("recv")
    b_lo, b_n = CUT, ROWS - CUT
    b_half = b_n // 2

    def ring_rows(part, way, s):
        lo, hi = PARTS[part]
        if s < 3:
            return lo, hi - lo
        half = (hi - lo) // 2
        return lo + way * half, half

    def origin(way, s):
        return chunk_at(lax.rem(z - s + NZ, NZ) if way == 0 else lax.rem(z + s, NZ))

    def z_sem(part, j, way, s):
        return (r_az + (j * 2 + way) * 4 + s) if part == 0 else (r_bz + way * 4 + s)

    def z_start(part, j, way, s):
        lo, n = ring_rows(part, way, s)
        here = w.at[origin(way, s), lax.rem(x - j + NX, NX), pl.ds(lo, n), :]
        send = s_az if part == 0 else s_bz
        copy(here, here, send, z_sem(part, j, way, s), zpeer(1 if way == 0 else NZ - 1)).start()

    def z_arrival(part, j, way, s):
        lo, n = ring_rows(part, way, s)
        arrived(w.at[origin(way, s + 1), lax.rem(x - j + NX, NX), pl.ds(lo, n), :], z_sem(part, j, way, s))

    sent(w.at[pl.ds(0, 7), :, pl.ds(0, CUT), :], s_az)
    sent(w.at[pl.ds(0, 7), 0, pl.ds(b_lo, b_n), :], s_bz)
    sent(w.at[pl.ds(0, 6), :, pl.ds(b_lo, b_n), :], s_bx)
    sent(w.at[0, pl.ds(0, 3), pl.ds(0, CUT), :], s_ax)

    def bx_sem(way, s):
        return r_bx + 3 * (0 if s == 0 else 1 + way * 3 + s - 1)

    def bx_start(way, s):
        here = w.at[origin(way, s), x, pl.ds(b_lo, b_n), :]
        for turn in range(2):
            copy(here, here, s_bx, bx_sem(way, s) + turn, xpeer(1 if turn == 0 else NX - 1)).start()

    def bx_forward(way, s):
        for turn in range(2):
            block = w.at[origin(way, s), lax.rem(x + (NX - 1 if turn == 0 else 1), NX)]
            arrived(block.at[pl.ds(b_lo, b_n), :], bx_sem(way, s) + turn)
            here = block.at[pl.ds(b_lo + turn * b_half, b_half), :]
            copy(here, here, s_bx, bx_sem(way, s) + 2, xpeer(1 if turn == 0 else NX - 1)).start()

    def bx_wait(way, s):
        arrived(w.at[origin(way, s), lax.rem(x + 2, NX), pl.ds(b_lo, b_n), :], bx_sem(way, s) + 2)

    def bx4_start(way):
        here = w.at[origin(way, 4), x, pl.ds(b_lo + way * b_half, b_half), :]
        each(1, NX, lambda d: copy(here, here, s_bx, r_bx4, xpeer(d)).start())

    def bx4_wait():
        arrived(w.at[0, pl.ds(0, 3), pl.ds(b_lo, b_n), :], r_bx4)

    r_sqx.wait()
    sqz[z] = total(sqx, NX)
    r_sqz.start(lambda _: sqz.at[z])
    wait_swap(1)
    for way in range(2):
        z_start(1, 0, way, 0)
    wait_swap(0)
    here_a = w.at[own, x, pl.ds(0, CUT), :]
    each(1, NX, lambda d: copy(here_a, here_a, s_ax, r_ax + d, xpeer(d)).start())
    for way in range(2):
        z_start(0, 0, way, 0)
    bx_start(0, 0)
    cot_start()
    arrived(actsf.at[others, :], r_acts)
    low_in = dot(ah[...], actsf[...], NT)
    r_sqz.wait()
    norms = jnp.sqrt(total(sqz, NZ)[0:1])
    ns[q, 0:1] = norms
    ns[q, 1:2] = mag[pl.ds(p, 1), :] / norms
    r_ns.start(lambda _: ns.at[q])
    for j in range(1, NX):
        arrived(w.at[own, lax.rem(x - j + NX, NX), pl.ds(0, CUT), :], r_ax + j)
        for way in range(2):
            z_start(0, j, way, 0)

    def ring_b(s):
        for way in range(2):
            z_arrival(1, 0, way, s - 1)
            if s < 4:
                z_start(1, 0, way, s)
                bx_start(way, s)
            else:
                bx4_start(way)

    def ring_a(s, *between):
        for j in range(NX):
            for way in range(2):
                z_arrival(0, j, way, s - 1)
                if s < 4:
                    z_start(0, j, way, s)
            if j < len(between):
                between[j]()

    def forward(zi):
        out = dot(actsf[...], w[zi].reshape(NX * ROWS, COLS))
        momt[pl.ds(zi, 1), :] = jnp.sum(out * gf[zi].astype(F32), axis=0, keepdims=True)

    r_tb = Ring(NQ, q, qpeer, tbi)
    r_ctz = Ring(NZ, z, zpeer, cti)
    r_ctx = Ring(NX, x, xpeer, ctx)
    r_ctg = Ring(NZ, z, zpeer, ctz)
    r_tpx = Ring(NX, x, xpeer, tpi)
    r_tpz = Ring(NZ, z, zpeer, tpzi)
    r_tpg = Ring(NZ, z, zpeer, tpg)

    def send_token_b():
        for k in range(2):
            parts = jnp.concatenate(pieces(low_in[k * RANK : (k + 1) * RANK], 3), axis=0)
            for yy in range(NY):
                t = dot(parts, gf[2 * yy + k])
                tbp[2 * yy + k] = t[0:RANK] + t[RANK : 2 * RANK] + t[2 * RANK :]
        tbi[q] = tbp[q]
        r_tb.start(lambda i: tbp.at[i])

    def send_tokens():
        r_ns.wait()
        low = []
        for k in range(2):
            acc = None
            for yy in range(NY):
                i = 2 * yy + k
                s = (gf[i].astype(F32) * ns[i, 1:2]).astype(BF16)
                scaled[i] = s
                t = dot(s, bf[yy, k], NT)
                acc = t if acc is None else acc + t
            low.append(acc)
        lowf = jnp.concatenate(low, axis=1)
        lowo[...] = lowf.astype(BF16)
        lowt = lowf.T.astype(BF16)
        for xx in range(NX):
            tpp[xx] = dot(lowt, actsf[:, xx * ROWS : (xx + 1) * ROWS])
        tpi[x] = tpp[x]
        r_tpx.start(lambda i: tpp.at[i])

    def sum_tokens_x():
        r_tpx.wait()
        tps[...] = total(tpi, NX).reshape(NZ, 8, ROWS)
        tpzi[z] = tps[z]
        r_tpz.start(lambda i: tps.at[i])

    def sum_tokens_z():
        r_tpz.wait()
        tpg[z] = total(tpzi, NZ)
        r_tpg.start(lambda _: tpg.at[z])

    def sum_products_q():
        r_tb.wait()
        token_b = total(tbi, NQ)
        for g in range(NZ):
            ctp[g, 0:4] = across[4 * g : 4 * g + 4]
            ctp[g, 4:8] = token_b[4 * g : 4 * g + 4]
        cti[z] = ctp[z]
        r_ctz.start(lambda i: ctp.at[i])

    def sum_products_z():
        r_ctz.wait()
        ctx[x] = total(cti, NZ)
        r_ctx.start(lambda _: ctx.at[x])

    def sum_products_x():
        r_ctx.wait()
        ctz[z] = total(ctx, NX)
        r_ctg.start(lambda _: ctz.at[z])

    def column_sums(way, s):
        bx_wait(way, s)
        forward(origin(way, s))

    ring_b(1)
    bx_forward(0, 0)
    ring_a(1, lambda: None, cot_relay)
    ring_b(2)
    bx_forward(0, 1)
    bx_forward(1, 1)
    r_b.wait()
    cot_wait()
    send_token_b()
    send_tokens()
    ring_a(2, lambda: column_sums(0, 0), lambda: None, sum_products_q)
    ring_b(3)
    bx_forward(0, 2)
    bx_forward(1, 2)
    sum_tokens_x()
    column_sums(0, 1)
    column_sums(1, 1)
    ring_a(3)
    ring_b(4)
    bx_forward(0, 3)
    bx_forward(1, 3)
    column_sums(0, 2)
    column_sums(1, 2)
    ring_a(4)
    column_sums(0, 3)
    column_sums(1, 3)
    bx4_wait()
    forward(origin(0, 4))

    r_mox = Ring(NX, x, xpeer, mox)
    r_moz = Ring(NZ, z, zpeer, moz)
    r_moq = Ring(NQ, q, qpeer, moq)
    extra = []
    for i in range(NQ):
        extra.append(jnp.sum(tbp[i] * bf[i // 2, i % 2].astype(F32), axis=0, keepdims=True))
    mox[x] = momt[...] + jnp.concatenate(extra, axis=0)
    r_mox.start(lambda _: mox.at[x])

    def backward(xx):
        acc = dot(lowo[...], ah[:, xx * ROWS : (xx + 1) * ROWS])
        for zi in range(NZ):
            acc = acc + dot(scaled[zi], w[zi, xx], NT)
        gxb[:, xx * ROWS : (xx + 1) * ROWS] = acc.astype(BF16)

    sum_tokens_z()
    sum_products_z()
    backward(0)
    r_mox.wait()
    moz[z] = total(mox, NX)
    r_moz.start(lambda _: moz.at[z])
    sum_products_x()
    backward(1)
    backward(2)
    r_moz.wait()
    moq[q] = total(moz, NZ)
    r_moq.start(lambda _: moq.at[q])
    r_ctg.wait()
    ctc[p] = ctz[...]
    s_ctc, r_ctc = sems("send"), sems("recv")
    copy(ctc.at[p], ctc.at[p], s_ctc, r_ctc, core).start()
    sent(ctc.at[p], s_ctc)
    backward(3)

    s_gx, r_gx = sems("send"), sems("recv")
    copy(gxb.at[others, :], gx_out.at[:, my_half], s_gx, r_gx, core).start()
    sent(gxb.at[others, :], s_gx)
    stores = [pltpu.make_async_copy(gxb.at[mine, :], gx_out.at[:, my_half], lsem.at[sems("local")])]
    stores[0].start()

    r_moq.wait()
    moment = total(moq, NQ)
    norm_all = jnp.concatenate([ns[i, 0:1] for i in range(NQ)], axis=0)
    scal_all = jnp.concatenate([ns[i, 1:2] for i in range(NQ)], axis=0)
    grad_mag = moment / norm_all
    factor = scal_all * grad_mag / norm_all
    momt[...] = grad_mag

    for k in range(2):
        inner = None
        for yy in range(NY):
            i = 2 * yy + k
            two = jnp.concatenate(pieces(bf[yy, k].astype(F32) * factor[i : i + 1], 2), axis=0)
            wts[i] = two
            t = dot(two, bf[yy, k], NT)
            inner = t if inner is None else inner + t
        inr[k] = jnp.concatenate(pieces(inner[0:RANK] + inner[RANK:], 2), axis=0)

    s_gay, s_gax, s_gac = sems("send"), sems("send"), sems("send")
    r_gay, r_gax, r_gac = sems("recv", NY), sems("recv", 3 * NY), sems("recv", NX)
    l_ga = sems("local")

    def ga_block(d, of_core, j):
        return gaf.at[2 * lax.rem(y - d + NY, NY) + of_core, lax.rem(x - j + NX, NX)]

    def ga_store(d, of_core, j):
        block = ga_block(d, of_core, j)
        first = (2 * lax.rem(y - d + NY, NY) + of_core) * HALF + lax.rem(x - j + NX, NX) * ROWS
        for k in range(2):
            dst = ga_out.at[k, :, pl.ds(pl.multiple_of(first, 128), ROWS)]
            pltpu.make_async_copy(block.at[pl.ds(k * RANK, RANK), :], dst, lsem.at[l_ga]).start()

    def ga_core(d, j):
        here = ga_block(d, p, j)
        copy(here, here, s_gac, r_gac + j, core).start()
        ga_store(d, p, j)

    def ga_x(d):
        here = ga_block(d, p, 0)
        for turn in range(2):
            copy(here, here, s_gax, r_gax + 3 * d + turn, xpeer(1 if turn == 0 else NX - 1)).start()
        ga_core(d, 0)

    r_tpg.wait()
    tokens = tpg[...].reshape(2 * RANK, ROWS)
    span = pl.ds(pl.multiple_of(x * ROWS, ROWS), ROWS)
    for k in range(2):
        acc = dot(inr[k], ah[k * RANK : (k + 1) * RANK, span])
        for yy in range(NY):
            acc = acc + dot(wts[2 * yy + k], w[2 * yy + k, x], NT)
        rows = slice(k * RANK, (k + 1) * RANK)
        gaf[q, x, rows, :] = (tokens[rows] - (acc[0:RANK] + acc[RANK:])).astype(BF16)
    here_ga = gaf.at[q, x]
    each(1, NY, lambda d: copy(here_ga, here_ga, s_gay, r_gay + d, ypeer(d)).start())
    ga_x(0)

    arrived(ctc.at[1 - p], r_ctc)
    for k in range(2):
        i = 2 * y + k
        norm_k = ns[i, 0:1]
        scal_k = ns[i, 1:2]
        gm_k = momt[pl.ds(i, 1), :]
        gm_out[k : k + 1] = gm_k
        ratio = gm_k / norm_k
        for g in range(NZ):
            gb_out[k, 4 * g : 4 * g + 4] = scal_k * (ctc[k, g, 4:8] - ctc[k, g, 0:4] * ratio)

    for d in (1, 3, 2):
        arrived(ga_block(d, p, 0), r_gay + d)
        ga_x(d)
    for d in (0, 1, 3, 2):
        for turn in range(2):
            j = 1 if turn == 0 else NX - 1
            here = ga_block(d, p, j)
            arrived(here, r_gax + 3 * d + turn)
            if (d in (0, 2)) == (turn == 0):
                copy(here, here, s_gax, r_gax + 3 * d + 2, xpeer(1 if turn == 0 else NX - 1)).start()
            ga_core(d, j)
    for d in (0, 1, 3, 2):
        arrived(ga_block(d, p, 2), r_gax + 3 * d + 2)
        ga_core(d, 2)
    for j in (0, 1, 3, 2):
        arrived(gaf.at[0], r_gac + j)
        for d in range(NY):
            ga_store(d, 1 - p, j)
    arrived(gxb.at[others, :], r_gx)
    for store in stores:
        store.wait()
    sent(gaf.at[0, pl.ds(0, 3)], s_gay)
    sent(gaf.at[pl.ds(0, 3)], s_gax)
    sent(gaf.at[pl.ds(0, NY)], s_gac)
    pltpu.make_async_copy(gaf, gaf, lsem.at[l_ga]).wait()
    assert counts == limits, counts
    for final in finals:
        final()


SENDS, RECVS, LOCALS = 27, 110, 9


def finish(gx, ga, gb, gm):
    cuts = 4

    def widen(gx_in, ga_in, gb_in, gm_in, gx_to, ga_to, gb_to, gm_to):
        gx_to[...] = gx_in[...]
        ga_to[...] = ga_in[...].astype(F32)
        gb_to[...] = gb_in[...]
        gm_to[...] = gm_in[...]

    specs = [
        pl.BlockSpec((TOK, FEAT // cuts), lambda i: (0, i)),
        pl.BlockSpec((2, RANK, NQ * HALF // cuts), lambda i: (0, 0, i)),
        pl.BlockSpec((2, RANK, COLS), lambda i: (0, 0, 0)),
        pl.BlockSpec((2, COLS), lambda i: (0, 0)),
    ]
    return pl.pallas_call(
        widen,
        grid=(cuts,),
        out_shape=tuple(
            jax.ShapeDtypeStruct(v.shape, F32 if v is ga else v.dtype) for v in (gx, ga, gb, gm)
        ),
        in_specs=specs,
        out_specs=tuple(specs),
        compiler_params=pltpu.CompilerParams(vmem_limit_bytes=62 * 2**20),
    )(gx, ga, gb, gm)


def on_device(acts, cot, base, adapter_a, adapter_b, magnitude):
    at = jnp.swapaxes(adapter_a, 1, 2)
    vm = pl.BlockSpec(memory_space=pltpu.VMEM)
    hbm = pl.BlockSpec(memory_space=pl.ANY)
    scratch = [
        ((NZ, NX, ROWS, COLS), BF16),
        ((TOK2, HALF), BF16),
        ((NQ, TOK2, COLS), BF16),
        ((NQ, TOK2, COLS), BF16),
        ((NY, 2, RANK, COLS), BF16),
        ((2 * RANK, HALF), BF16),
        ((RANK, ROWS), BF16),
        ((ROWS, COLS), BF16),
        ((NX, 8, COLS), F32),
        ((NZ, 8, COLS), F32),
        ((NQ, 8, COLS), F32),
        ((NQ, RANK, COLS), F32),
        ((NQ, RANK, COLS), F32),
        ((NZ, 8, COLS), F32),
        ((NZ, 8, COLS), F32),
        ((NX, 8, COLS), F32),
        ((NZ, 8, COLS), F32),
        ((2, NZ, 8, COLS), F32),
        ((NX, 2 * RANK, ROWS), F32),
        ((NX, 2 * RANK, ROWS), F32),
        ((NZ, 8, ROWS), F32),
        ((NZ, 8, ROWS), F32),
        ((NZ, 8, ROWS), F32),
        ((NX, 8, COLS), F32),
        ((NZ, 8, COLS), F32),
        ((NQ, 8, COLS), F32),
        ((NQ, NX, 2 * RANK, ROWS), BF16),
        ((TOK2, HALF), BF16),
        ((TOK2, 2 * RANK), BF16),
        ((NQ, COLS), F32),
        ((NQ, 2 * RANK, COLS), BF16),
        ((2, 2 * RANK, RANK), BF16),
    ]
    gx, ga, gb, gm = pl.pallas_call(
        kernel,
        out_shape=(
            jax.ShapeDtypeStruct((TOK, FEAT), BF16),
            jax.ShapeDtypeStruct((2, RANK, NQ * HALF), BF16),
            jax.ShapeDtypeStruct((2, RANK, COLS), F32),
            jax.ShapeDtypeStruct((2, COLS), F32),
        ),
        in_specs=[hbm, hbm, hbm, hbm, vm, vm],
        out_specs=(hbm, hbm, vm, vm),
        scratch_shapes=[pltpu.VMEM(shape, dtype) for shape, dtype in scratch]
        + [pltpu.SemaphoreType.DMA((n,)) for n in (SENDS, RECVS, LOCALS)],
        compiler_params=pltpu.CompilerParams(
            collective_id=0, has_side_effects=True, vmem_limit_bytes=56 * 2**20
        ),
        cost_estimate=pl.CostEstimate(flops=5 * 10**9, bytes_accessed=8 * 10**6, transcendentals=0),
    )(acts, cot, base, at, adapter_b, magnitude)
    gx, ga, gb, gm = finish(gx, ga, gb, gm)
    return gx, jnp.swapaxes(ga, 1, 2), gb, gm


def solution(mesh):
    in_specs = (
        P(("dp", "fsdp"), "col"),
        P(None, ("dp", "fsdp"), "col"),
        P(None, "fsdp", "col"),
        P(),
        P(None, None, "col"),
        P(None, "col"),
    )
    out_specs = (P(("dp", "fsdp"), "col"), P(), P(None, None, "col"), P(None, "col"))
    return jax.shard_map(
        on_device, mesh=mesh, in_specs=in_specs, out_specs=out_specs, check_vma=False
    )
```

```python
import functools

import jax
import jax.numpy as jnp
from jax import lax
from jax.experimental import pallas as pl
from jax.experimental.pallas import tpu as pltpu
from jax.sharding import PartitionSpec as P

MESH = pl.DeviceIdType.MESH
F32 = jnp.float32
BF16 = jnp.bfloat16

NX, NZ, NY = 4, 8, 4
NQ = 2 * NY

TOK = 192
PAIR = 4 * TOK
FEAT = 3072
HALF = FEAT // 2
COLS = 256
ROWS = 384
WORK = 2 * ROWS
RANK = 32
CUT = 160

NT = (((1,), (1,)), ((), ()))
TN = (((0,), (0,)), ((), ()))
NN = (((1,), (0,)), ((), ()))


def dot(a, b, dims=NN):
    return lax.dot_general(a, b, dims, preferred_element_type=F32)


def pieces(value, count):
    out = []
    for _ in range(count):
        part = value.astype(BF16)
        out.append(part)
        value = value - part.astype(F32)
    return out


def total(ref, count):
    value = ref[0]
    for i in range(1, count):
        value = value + ref[i]
    return value


def kernel(
    acts, cot, base, at, b, mag,
    gx_out, ga_out, gb_out, gm_out,
    w, actsf, gf, scaled, bf, ah, ar, mybase,
    sqx, sqz, ns, tbp, tbi, ctp, cti, ctx, ctz, ctc,
    tpp, tpi, tps, tpzi, tpg, mox, moz, moq, gaf, gxb, lowo, momt, wts, inr,
    ssem, rsem, lsem,
):
    p = lax.axis_index("dp")
    f = lax.axis_index("fsdp")
    y = lax.axis_index("col")
    x = lax.rem(f, NX)
    z = lax.div(f, NX)
    q = 2 * y + p

    def at_xz(nx, nz):
        return (p, nz * NX + nx, y)

    def at_q(nq):
        return (lax.rem(nq, 2), f, lax.div(nq, 2))

    xpeer = lambda d: at_xz(lax.rem(x + d, NX), z)
    zpeer = lambda d: at_xz(x, lax.rem(z + d, NZ))
    qpeer = lambda d: at_q(lax.rem(q + d, NQ))
    ypeer = lambda d: (p, f, lax.rem(y + d, NY))
    core = (1 - p, f, y)
    h = lax.rem(lax.div(x + 1, 2), 2)
    partner = (p, f + 1 - 2 * lax.rem(x, 2), y)
    cross = (1 - p, f + 1 - 2 * lax.rem(x, 2), y)
    across_x = at_xz(NX - 1 - x, z)
    own_slot = lax.div(x, 2)
    slot_of = lambda jj: lax.rem(own_slot + jj, 2)

    def shift(c):
        k, half = lax.rem(c, 2), lax.div(c, 2)
        return lax.rem((1 - k) * half + k * (4 + (4 - half) * jnp.minimum(half, 1)), NZ)

    def chunk_at(position):
        step = lax.rem(position - q + NZ, NZ)
        far = lax.div(step, 4)
        return (1 - far) * 2 * step + far * lax.rem(17 - 2 * step, NZ)

    target = (lax.rem(z, 2), lax.rem(z + shift(q), NZ) * NX + x, lax.div(z, 2))
    own = chunk_at(z)
    source = (lax.rem(own, 2), q * NX + x, lax.div(own, 2))
    fixed = jnp.logical_and(own == q, z == q)

    counts = {"send": 0, "recv": 0, "local": 0}
    limits = {"send": SENDS, "recv": RECVS, "local": LOCALS}
    finals = []

    def sems(kind, n=1):
        counts[kind] += n
        assert counts[kind] <= limits[kind]
        return counts[kind] - n

    def copy(src, dst, send, recv, dev):
        return pltpu.make_async_remote_copy(
            src_ref=src, dst_ref=dst, send_sem=ssem.at[send], recv_sem=rsem.at[recv],
            device_id=dev, device_id_type=MESH,
        )

    def arrived(ref, recv):
        copy(ref, ref, 0, recv, core).wait_recv()

    def sent(ref, send):
        finals.append(lambda: copy(ref, ref, send, 0, core).wait_send())

    def each(lo, hi, body):
        def step(i, carry):
            body(i)
            return carry

        lax.fori_loop(lo, hi, step, 0)

    class Ring:
        def __init__(self, n, me, peer, dst):
            self.n, self.me, self.peer, self.dst = n, me, peer, dst
            self.send, self.recv = sems("send"), sems("recv")

        def start(self, src):
            def one(d):
                block = src(lax.rem(self.me + d, self.n))
                copy(block, self.dst.at[self.me], self.send, self.recv, self.peer(d)).start()

            each(1, self.n, one)
            sent(self.dst.at[pl.ds(0, self.n - 1)], self.send)

        def wait(self):
            arrived(self.dst.at[pl.ds(0, self.n - 1)], self.recv)

    def tokens_of(core_of, half_of):
        return pl.ds(pl.multiple_of(core_of * 2 * TOK + half_of * TOK, TOK), TOK)

    mine = tokens_of(p, h)
    my_core = pl.ds(pl.multiple_of(p * 2 * TOK, TOK), 2 * TOK)

    def shard(core_of, half_of, j):
        return pl.ds(pl.multiple_of(core_of * HALF + (half_of + j * (3 - 2 * half_of)) * ROWS, 128), ROWS)

    bar = pltpu.get_barrier_semaphore()
    each(1, NX, lambda d: pl.semaphore_signal(bar, inc=1, device_id=xpeer(d), device_id_type=MESH))
    each(1, NZ, lambda d: pl.semaphore_signal(bar, inc=1, device_id=zpeer(d), device_id_type=MESH))
    each(1, NQ, lambda d: pl.semaphore_signal(bar, inc=1, device_id=qpeer(d), device_id_type=MESH))

    pl.semaphore_signal(bar, inc=1, device_id=cross, device_id_type=MESH)

    @pl.when(jnp.logical_not(fixed))
    def _():
        pl.semaphore_signal(bar, inc=1, device_id=source, device_id_type=MESH)

    loads = [
        pltpu.make_async_copy(base.at[p], mybase, lsem.at[sems("local")]),
        pltpu.make_async_copy(at.at[p, :, pl.ds(pl.multiple_of(f * ROWS, ROWS), ROWS)], ar, lsem.at[sems("local")]),
    ]
    for k in range(2):
        for j in range(2):
            cols = pl.ds(pl.multiple_of(q * HALF + (h + j * (3 - 2 * h)) * ROWS, 128), ROWS)
            dst = ah.at[pl.ds(k * RANK, RANK), pl.ds(j * ROWS, ROWS)]
            loads.append(pltpu.make_async_copy(at.at[k, :, cols], dst, lsem.at[sems("local")]))
        loads.append(pltpu.make_async_copy(cot.at[k], gf.at[2 * y + k, mine, :], lsem.at[sems("local")]))
    for j in range(2):
        dst = actsf.at[mine, pl.ds(j * ROWS, ROWS)]
        loads.append(pltpu.make_async_copy(acts.at[:, shard(p, h, j)], dst, lsem.at[sems("local")]))
    for load in loads:
        load.start()

    @pl.when(jnp.logical_not(fixed))
    def _():
        pl.semaphore_wait(bar, NX + NZ + NQ - 1)

    @pl.when(fixed)
    def _():
        pl.semaphore_wait(bar, NX + NZ + NQ - 2)

    PARTS = ((0, CUT), (CUT, ROWS))
    s_swap, r_swap = sems("send"), sems("recv", 2)

    def swap_copy(i):
        lo, hi = PARTS[i]
        return copy(base.at[p, pl.ds(lo, hi - lo), :], w.at[q, own_slot, pl.ds(lo, hi - lo), :], s_swap, r_swap + i, target)

    @pl.when(jnp.logical_not(fixed))
    def _():
        swap_copy(1).start()
        swap_copy(0).start()

    def wait_swap(i):
        lo, hi = PARTS[i]

        @pl.when(jnp.logical_not(fixed))
        def _():
            arrived(w.at[own, own_slot, pl.ds(lo, hi - lo), :], r_swap + i)

        @pl.when(fixed)
        def _():
            w[own, own_slot, lo:hi, :] = mybase[lo:hi, :]

    def final_swap():
        @pl.when(jnp.logical_not(fixed))
        def _():
            copy(mybase, mybase, s_swap, 0, target).wait_send()

    finals.append(final_swap)
    r_sqx = Ring(NX, x, xpeer, sqx)
    r_sqz = Ring(NZ, z, zpeer, sqz)
    r_ns = Ring(NQ, q, qpeer, ns)
    for load in loads:
        load.wait()
    composed = mybase[...].astype(F32) + dot(ar[...], b[p], TN)
    sqx[x] = jnp.broadcast_to(jnp.sum(composed * composed, axis=0, keepdims=True), (8, COLS))
    across = functools.reduce(lambda u, v: u + v, [dot(ar[...], c) for c in pieces(composed, 3)])

    r_sqx.start(lambda _: sqx.at[x])

    s_gotx, s_goty, s_gotc = sems("send"), sems("send"), sems("send")
    r_gotx, r_goty, r_gotc = sems("recv"), sems("recv", 6), sems("recv")
    parts_of_pair = (mine, tokens_of(p, 1 - h))
    two = gf.at[0, my_core, :]
    def cot_y(i, source=None):
        for turn in range(2):
            for k in range(2):
                there = gf.at[2 * y + k, parts_of_pair[i], :]
                src = there if source is None else source.at[k]
                copy(src, there, s_goty, r_goty + 3 * i + turn, ypeer(1 if turn == 0 else NY - 1)).start()

    def cot_forward(i):
        for turn in range(2):
            arrived(two, r_goty + 3 * i + turn)
            yy = lax.rem(y + (NY - 1 if turn == 0 else 1), NY)
            here = gf.at[2 * yy + turn, parts_of_pair[i], :]
            copy(here, here, s_goty, r_goty + 3 * i + 2, ypeer(1 if turn == 0 else NY - 1)).start()

    def cot_core(d):
        for k in range(2):
            here = gf.at[2 * lax.rem(y - d + NY, NY) + k, my_core, :]
            copy(here, here, s_gotc, r_gotc, core).start()

    cot_y(0, cot)
    for k in range(2):
        copy(cot.at[k], gf.at[2 * y + k, mine, :], s_gotx, r_gotx, partner).start()
    sent(two, s_gotx)

    sent(gf.at[pl.ds(0, NY - 1)], s_goty)
    sent(gf.at[pl.ds(0, NY)], s_gotc)

    def cot_start():
        arrived(two, r_gotx)
        cot_y(1)
        cot_core(0)

    def cot_relay():
        cot_forward(1)
        cot_core(1)
        cot_core(3)

    def cot_relay_last():
        for i in range(2):
            arrived(two, r_goty + 3 * i + 2)
        cot_core(2)

    def cot_wait():
        arrived(gf.at[pl.ds(0, NY)], r_gotc)

    s_acts, r_acts = sems("send"), sems("recv")

    def acts_start(j):
        for core_of, half_of, dev in ((p, 1 - h, partner), (1 - p, 1 - h, cross), (1 - p, h, core)):
            dst = actsf.at[mine, pl.ds(j * ROWS, ROWS)]
            copy(acts.at[:, shard(core_of, half_of, j)], dst, s_acts, r_acts, dev).start()

    acts_start(0)
    sent(actsf.at[pl.ds(0, 3 * TOK), :], s_acts)

    def acts_wait():
        arrived(actsf.at[pl.ds(0, 3 * TOK), :], r_acts)

    r_b = Ring(NY, y, ypeer, bf)
    bf[y] = b[...]
    r_b.start(lambda i: bf.at[y])

    s_ax, s_az, s_bz, s_bx = sems("send"), sems("send"), sems("send"), sems("send")
    r_ax, r_az, r_bz = sems("recv"), sems("recv", 2 * 8), sems("recv", 8)
    r_bx, r_bx4 = sems("recv", 7), sems("recv")
    b_lo, b_n = CUT, ROWS - CUT
    b_half = b_n // 2

    def ring_rows(part, way, s):
        lo, hi = PARTS[part]
        if s < 3:
            return lo, hi - lo
        half = (hi - lo) // 2
        return lo + way * half, half

    def origin(way, s):
        return chunk_at(lax.rem(z - s + NZ, NZ) if way == 0 else lax.rem(z + s, NZ))

    def z_sem(part, j, way, s):
        return (r_az + (j * 2 + way) * 4 + s) if part == 0 else (r_bz + way * 4 + s)

    def z_start(part, j, way, s):
        lo, n = ring_rows(part, way, s)
        here = w.at[origin(way, s), slot_of(j), pl.ds(lo, n), :]
        send = s_az if part == 0 else s_bz
        copy(here, here, send, z_sem(part, j, way, s), zpeer(1 if way == 0 else NZ - 1)).start()

    def z_arrival(part, j, way, s):
        lo, n = ring_rows(part, way, s)
        arrived(w.at[origin(way, s + 1), slot_of(j), pl.ds(lo, n), :], z_sem(part, j, way, s))

    sent(w.at[pl.ds(0, 7), :, pl.ds(0, CUT), :], s_az)
    sent(w.at[pl.ds(0, 7), 0, pl.ds(b_lo, b_n), :], s_bz)
    sent(w.at[pl.ds(0, 4), :, pl.ds(b_lo, b_n), :], s_bx)
    sent(w.at[0, 0, pl.ds(0, CUT), :], s_ax)

    def bx_sem(way, s):
        return r_bx + (0 if s == 0 else 1 + way * 3 + s - 1)

    def bx_start(way, s):
        here = w.at[origin(way, s), own_slot, pl.ds(b_lo, b_n), :]
        copy(here, here, s_bx, bx_sem(way, s), across_x).start()

    def bx_wait(way, s):
        arrived(w.at[origin(way, s), slot_of(1), pl.ds(b_lo, b_n), :], bx_sem(way, s))

    def bx4_start(way):
        here = w.at[origin(way, 4), own_slot, pl.ds(b_lo + way * b_half, b_half), :]
        copy(here, here, s_bx, r_bx4, across_x).start()

    def bx4_wait():
        arrived(w.at[origin(0, 4), slot_of(1), pl.ds(b_lo, b_n), :], r_bx4)

    r_sqx.wait()
    sqz[z] = total(sqx, NX)
    r_sqz.start(lambda _: sqz.at[z])
    cot_start()
    wait_swap(1)
    for way in range(2):
        z_start(1, 0, way, 0)
    wait_swap(0)
    here_a = w.at[own, own_slot, pl.ds(0, CUT), :]
    copy(here_a, here_a, s_ax, r_ax, across_x).start()
    for way in range(2):
        z_start(0, 0, way, 0)
    bx_start(0, 0)
    acts_start(1)
    cot_forward(0)
    r_sqz.wait()
    norms = jnp.sqrt(total(sqz, NZ)[0:1])
    ns[q, 0:1] = norms
    ns[q, 1:2] = mag[pl.ds(p, 1), :] / norms
    r_ns.start(lambda _: ns.at[q])
    def ring_b(s):
        for way in range(2):
            z_arrival(1, 0, way, s - 1)
            if s < 4:
                z_start(1, 0, way, s)
                bx_start(way, s)
            else:
                bx4_start(way)

    def ring_a(j, s):
        for way in range(2):
            z_arrival(0, j, way, s - 1)
            if s < 4:
                z_start(0, j, way, s)

    def forward(zi):
        out = dot(actsf[...], w[zi].reshape(WORK, COLS))
        momt[pl.ds(zi, 1), :] = jnp.sum(out * gf[zi].astype(F32), axis=0, keepdims=True)

    r_tb = Ring(NQ, q, qpeer, tbi)
    r_ctz = Ring(NZ, z, zpeer, cti)
    r_ctx = Ring(NX, x, xpeer, ctx)
    r_ctg = Ring(NZ, z, zpeer, ctz)
    s_tpx, r_tpx = sems("send"), sems("recv")
    r_tpz = Ring(NZ, z, zpeer, tpzi)
    r_tpg = Ring(NZ, z, zpeer, tpg)

    def send_token_b():
        low_in = dot(ah[...], actsf[...], NT)
        for k in range(2):
            parts = jnp.concatenate(pieces(low_in[k * RANK : (k + 1) * RANK], 3), axis=0)
            for yy in range(NY):
                t = dot(parts, gf[2 * yy + k])
                tbp[2 * yy + k] = t[0:RANK] + t[RANK : 2 * RANK] + t[2 * RANK :]
        tbi[q] = tbp[q]
        r_tb.start(lambda i: tbp.at[i])

    def send_tokens():
        r_ns.wait()
        low = []
        for k in range(2):
            acc = None
            for yy in range(NY):
                i = 2 * yy + k
                s = (gf[i].astype(F32) * ns[i, 1:2]).astype(BF16)
                scaled[i] = s
                t = dot(s, bf[yy, k], NT)
                acc = t if acc is None else acc + t
            low.append(acc)
        lowf = jnp.concatenate(low, axis=1)
        lowo[...] = lowf.astype(BF16)
        lowt = lowf.T.astype(BF16)
        for j in range(2):
            tpp[j] = dot(lowt, actsf[:, j * ROWS : (j + 1) * ROWS])
        copy(tpp.at[slot_of(1)], tpi, s_tpx, r_tpx, across_x).start()
        sent(tpi, s_tpx)

    def sum_tokens_x():
        arrived(tpi, r_tpx)
        tps[...] = (tpp[own_slot] + tpi[...]).reshape(NZ, 8, ROWS)
        tpzi[z] = tps[z]
        r_tpz.start(lambda i: tps.at[i])

    def sum_tokens_z():
        r_tpz.wait()
        tpg[z] = total(tpzi, NZ)
        r_tpg.start(lambda _: tpg.at[z])

    def sum_products_q():
        r_tb.wait()
        token_b = total(tbi, NQ)
        for g in range(NZ):
            ctp[g, 0:4] = across[4 * g : 4 * g + 4]
            ctp[g, 4:8] = token_b[4 * g : 4 * g + 4]
        cti[z] = ctp[z]
        r_ctz.start(lambda i: ctp.at[i])

    def sum_products_z():
        r_ctz.wait()
        ctx[x] = total(cti, NZ)
        r_ctx.start(lambda _: ctx.at[x])

    def sum_products_x():
        r_ctx.wait()
        ctz[z] = total(ctx, NX)
        r_ctg.start(lambda _: ctz.at[z])

    def column_sums(way, s):
        bx_wait(way, s)
        forward(origin(way, s))

    ring_b(1)
    ring_a(0, 1)
    arrived(w.at[own, slot_of(1), pl.ds(0, CUT), :], r_ax)
    for way in range(2):
        z_start(0, 1, way, 0)
    cot_relay()
    ring_b(2)
    ring_a(0, 2)
    ring_a(1, 1)
    r_b.wait()
    cot_relay_last()
    cot_wait()
    acts_wait()
    send_tokens()
    ring_b(3)
    ring_a(0, 3)
    column_sums(0, 0)
    send_token_b()
    ring_a(1, 2)
    column_sums(0, 1)
    column_sums(1, 1)
    ring_b(4)
    ring_a(0, 4)
    column_sums(0, 2)
    column_sums(1, 2)
    ring_a(1, 3)
    column_sums(0, 3)
    column_sums(1, 3)
    sum_tokens_x()
    sum_products_q()
    ring_a(1, 4)
    bx4_wait()
    forward(origin(0, 4))

    r_mox = Ring(NX, x, xpeer, mox)
    r_moz = Ring(NZ, z, zpeer, moz)
    r_moq = Ring(NQ, q, qpeer, moq)
    extra = []
    for i in range(NQ):
        extra.append(jnp.sum(tbp[i] * bf[i // 2, i % 2].astype(F32), axis=0, keepdims=True))
    mox[x] = momt[...] + jnp.concatenate(extra, axis=0)
    r_mox.start(lambda _: mox.at[x])

    s_gx, r_gx = sems("send"), sems("recv")
    l_gx = sems("local")

    def backward(j):
        cols = slice(j * ROWS, (j + 1) * ROWS)
        acc = dot(lowo[...], ah[:, cols])
        for zi in range(NZ):
            acc = acc + dot(scaled[zi], w[zi, j], NT)
        gxb[:, cols] = acc.astype(BF16)
        there = gx_out.at[:, shard(p, h, j)]
        part = pl.ds(j * ROWS, ROWS)
        for core_of, half_of, dev in ((p, 1 - h, partner), (1 - p, 1 - h, cross), (1 - p, h, core)):
            copy(gxb.at[tokens_of(core_of, half_of), part], there, s_gx, r_gx, dev).start()
        pltpu.make_async_copy(gxb.at[mine, part], there, lsem.at[l_gx]).start()

    backward(0)
    r_mox.wait()
    moz[z] = total(mox, NX)
    r_moz.start(lambda _: moz.at[z])
    backward(1)
    sum_tokens_z()
    r_moz.wait()
    moq[q] = total(moz, NZ)
    r_moq.start(lambda _: moq.at[q])
    sum_products_z()
    r_moq.wait()
    moment = total(moq, NQ)
    norm_all = jnp.concatenate([ns[i, 0:1] for i in range(NQ)], axis=0)
    scal_all = jnp.concatenate([ns[i, 1:2] for i in range(NQ)], axis=0)
    grad_mag = moment / norm_all
    factor = scal_all * grad_mag / norm_all
    momt[...] = grad_mag

    for k in range(2):
        inner = None
        for yy in range(NY):
            i = 2 * yy + k
            two = jnp.concatenate(pieces(bf[yy, k].astype(F32) * factor[i : i + 1], 2), axis=0)
            wts[i] = two
            t = dot(two, bf[yy, k], NT)
            inner = t if inner is None else inner + t
        inr[k] = jnp.concatenate(pieces(inner[0:RANK] + inner[RANK:], 2), axis=0)

    s_gay, s_gax, s_gac = sems("send"), sems("send"), sems("send")
    r_gay, r_gax, r_gac = sems("recv", NY), sems("recv", 3 * NY), sems("recv", NX)
    l_ga = sems("local")

    def ga_block(d, of_core, j):
        return gaf.at[2 * lax.rem(y - d + NY, NY) + of_core, lax.rem(x - j + NX, NX)]

    def ga_store(d, of_core, j):
        block = ga_block(d, of_core, j)
        first = (2 * lax.rem(y - d + NY, NY) + of_core) * HALF + lax.rem(x - j + NX, NX) * ROWS
        for k in range(2):
            dst = ga_out.at[k, :, pl.ds(pl.multiple_of(first, 128), ROWS)]
            pltpu.make_async_copy(block.at[pl.ds(k * RANK, RANK), :], dst, lsem.at[l_ga]).start()

    def ga_core(d, j):
        here = ga_block(d, p, j)
        copy(here, here, s_gac, r_gac + j, core).start()
        ga_store(d, p, j)

    def ga_x(d):
        here = ga_block(d, p, 0)
        for turn in range(2):
            copy(here, here, s_gax, r_gax + 3 * d + turn, xpeer(1 if turn == 0 else NX - 1)).start()
        ga_core(d, 0)

    r_tpg.wait()
    tokens = tpg[...].reshape(2 * RANK, ROWS)
    span = pl.ds(pl.multiple_of(own_slot * ROWS, 128), ROWS)
    for k in range(2):
        acc = dot(inr[k], ah[k * RANK : (k + 1) * RANK, span])
        for yy in range(NY):
            acc = acc + dot(wts[2 * yy + k], w[2 * yy + k, own_slot], NT)
        rows = slice(k * RANK, (k + 1) * RANK)
        gaf[q, x, rows, :] = (tokens[rows] - (acc[0:RANK] + acc[RANK:])).astype(BF16)
    here_ga = gaf.at[q, x]
    each(1, NY, lambda d: copy(here_ga, here_ga, s_gay, r_gay + d, ypeer(d)).start())
    ga_x(0)

    for d in (1, 3, 2):
        arrived(ga_block(d, p, 0), r_gay + d)
        ga_x(d)
    sum_products_x()
    for d in (0, 1, 3, 2):
        for turn in range(2):
            j = 1 if turn == 0 else NX - 1
            here = ga_block(d, p, j)
            arrived(here, r_gax + 3 * d + turn)
            if (d in (0, 2)) == (turn == 0):
                copy(here, here, s_gax, r_gax + 3 * d + 2, xpeer(1 if turn == 0 else NX - 1)).start()
            ga_core(d, j)
    r_ctg.wait()
    ctc[p] = ctz[...]
    s_ctc, r_ctc = sems("send"), sems("recv")
    copy(ctc.at[p], ctc.at[p], s_ctc, r_ctc, core).start()
    sent(ctc.at[p], s_ctc)
    for d in (0, 1, 3, 2):
        arrived(ga_block(d, p, 2), r_gax + 3 * d + 2)
        ga_core(d, 2)
    arrived(ctc.at[1 - p], r_ctc)
    for k in range(2):
        i = 2 * y + k
        norm_k = ns[i, 0:1]
        scal_k = ns[i, 1:2]
        gm_k = momt[pl.ds(i, 1), :]
        gm_out[k : k + 1] = gm_k
        ratio = gm_k / norm_k
        for g in range(NZ):
            gb_out[k, 4 * g : 4 * g + 4] = scal_k * (ctc[k, g, 4:8] - ctc[k, g, 0:4] * ratio)

    for j in (0, 1, 3, 2):
        arrived(gaf.at[0], r_gac + j)
        for d in range(NY):
            ga_store(d, 1 - p, j)
    arrived(gxb.at[pl.ds(0, 3 * TOK), :], r_gx)
    sent(gxb.at[pl.ds(0, 3 * TOK), :], s_gx)
    pltpu.make_async_copy(gxb.at[mine, :], gxb.at[mine, :], lsem.at[l_gx]).wait()
    sent(gaf.at[0, pl.ds(0, 3)], s_gay)
    sent(gaf.at[pl.ds(0, 3)], s_gax)
    sent(gaf.at[pl.ds(0, NY)], s_gac)
    pltpu.make_async_copy(gaf, gaf, lsem.at[l_ga]).wait()
    assert counts == limits, counts
    for final in finals:
        final()


SENDS, RECVS, LOCALS = 28, 80, 12


def finish(gx, ga, gb, gm):
    cuts = 8
    wide = NQ * HALF // cuts
    tall = TOK // 4

    def widen(gx_in, ga_in, gb_in, gm_in, gx_to, ga_to, gb_to, gm_to, narrow, full, held, sem, out_sem, gx_sem):
        def load(i):
            return pltpu.make_async_copy(ga_in.at[:, :, pl.ds(i * wide, wide)], narrow.at[i], sem.at[i])

        for i in range(cuts):
            load(i).start()
        def pick(i):
            return pltpu.make_async_copy(gx_in.at[pl.ds(i * tall, tall), :], held.at[i], gx_sem.at[i])

        for i in range(4):
            pick(i).start()
        gb_to[...] = gb_in[...]
        gm_to[...] = gm_in[...]
        for i in range(cuts):
            load(i).wait()
            full[i] = narrow[i].astype(F32)
            pltpu.make_async_copy(full.at[i], ga_to.at[:, :, pl.ds(i * wide, wide)], out_sem).start()
        for i in range(4):
            pick(i).wait()
            pltpu.make_async_copy(held.at[i], gx_to.at[pl.ds(i * tall, tall), :], gx_sem.at[4]).start()
        pltpu.make_async_copy(full, full, out_sem).wait()
        pltpu.make_async_copy(held, held, gx_sem.at[4]).wait()

    vm = pl.BlockSpec(memory_space=pltpu.VMEM)
    hbm = pl.BlockSpec(memory_space=pl.ANY)
    return pl.pallas_call(
        widen,
        out_shape=tuple(
            jax.ShapeDtypeStruct(v.shape, F32 if v is ga else v.dtype) for v in (gx, ga, gb, gm)
        ),
        in_specs=[hbm, hbm, vm, vm],
        out_specs=(hbm, hbm, vm, vm),
        scratch_shapes=[
            pltpu.VMEM((cuts, 2, RANK, wide), BF16),
            pltpu.VMEM((cuts, 2, RANK, wide), F32),
            pltpu.VMEM((4, tall, FEAT), BF16),
            pltpu.SemaphoreType.DMA((cuts,)),
            pltpu.SemaphoreType.DMA,
            pltpu.SemaphoreType.DMA((5,)),
        ],
        compiler_params=pltpu.CompilerParams(vmem_limit_bytes=62 * 2**20),
    )(gx, ga, gb, gm)


def on_device(acts, cot, base, adapter_a, adapter_b, magnitude):
    at = jnp.swapaxes(adapter_a, 1, 2)
    vm = pl.BlockSpec(memory_space=pltpu.VMEM)
    hbm = pl.BlockSpec(memory_space=pl.ANY)
    scratch = [
        ((NZ, 2, ROWS, COLS), BF16),
        ((PAIR, WORK), BF16),
        ((NQ, PAIR, COLS), BF16),
        ((NQ, PAIR, COLS), BF16),
        ((NY, 2, RANK, COLS), BF16),
        ((2 * RANK, WORK), BF16),
        ((RANK, ROWS), BF16),
        ((ROWS, COLS), BF16),
        ((NX, 8, COLS), F32),
        ((NZ, 8, COLS), F32),
        ((NQ, 8, COLS), F32),
        ((NQ, RANK, COLS), F32),
        ((NQ, RANK, COLS), F32),
        ((NZ, 8, COLS), F32),
        ((NZ, 8, COLS), F32),
        ((NX, 8, COLS), F32),
        ((NZ, 8, COLS), F32),
        ((2, NZ, 8, COLS), F32),
        ((2, 2 * RANK, ROWS), F32),
        ((2 * RANK, ROWS), F32),
        ((NZ, 8, ROWS), F32),
        ((NZ, 8, ROWS), F32),
        ((NZ, 8, ROWS), F32),
        ((NX, 8, COLS), F32),
        ((NZ, 8, COLS), F32),
        ((NQ, 8, COLS), F32),
        ((NQ, NX, 2 * RANK, ROWS), BF16),
        ((PAIR, WORK), BF16),
        ((PAIR, 2 * RANK), BF16),
        ((NQ, COLS), F32),
        ((NQ, 2 * RANK, COLS), BF16),
        ((2, 2 * RANK, RANK), BF16),
    ]
    gx, ga, gb, gm = pl.pallas_call(
        kernel,
        out_shape=(
            jax.ShapeDtypeStruct((TOK, FEAT), BF16),
            jax.ShapeDtypeStruct((2, RANK, NQ * HALF), BF16),
            jax.ShapeDtypeStruct((2, RANK, COLS), F32),
            jax.ShapeDtypeStruct((2, COLS), F32),
        ),
        in_specs=[hbm, hbm, hbm, hbm, vm, vm],
        out_specs=(hbm, hbm, vm, vm),
        scratch_shapes=[pltpu.VMEM(shape, dtype) for shape, dtype in scratch]
        + [pltpu.SemaphoreType.DMA((n,)) for n in (SENDS, RECVS, LOCALS)],
        compiler_params=pltpu.CompilerParams(
            collective_id=0, has_side_effects=True, vmem_limit_bytes=56 * 2**20
        ),
        cost_estimate=pl.CostEstimate(flops=5 * 10**9, bytes_accessed=8 * 10**6, transcendentals=0),
    )(acts, cot, base, at, adapter_b, magnitude)
    gx, ga, gb, gm = finish(gx, ga, gb, gm)
    return gx, jnp.swapaxes(ga, 1, 2), gb, gm


def solution(mesh):
    in_specs = (
        P(("dp", "fsdp"), "col"),
        P(None, ("dp", "fsdp"), "col"),
        P(None, "fsdp", "col"),
        P(),
        P(None, None, "col"),
        P(None, "col"),
    )
    out_specs = (P(("dp", "fsdp"), "col"), P(), P(None, None, "col"), P(None, "col"))
    return jax.shard_map(
        on_device, mesh=mesh, in_specs=in_specs, out_specs=out_specs, check_vma=False
    )
```

```python
import functools

import jax
import jax.numpy as jnp
from jax import lax
from jax.experimental import pallas as pl
from jax.experimental.pallas import tpu as pltpu
from jax.sharding import PartitionSpec as P

MESH = pl.DeviceIdType.MESH
F32 = jnp.float32
BF16 = jnp.bfloat16

NX, NZ, NY = 4, 8, 4
NQ = 2 * NY

TOK = 192
PAIR = 4 * TOK
FEAT = 3072
HALF = FEAT // 2
COLS = 256
ROWS = 384
WORK = 2 * ROWS
RANK = 32
TILE = 128
CUT = 160

NT = (((1,), (1,)), ((), ()))
TN = (((0,), (0,)), ((), ()))
NN = (((1,), (0,)), ((), ()))


def dot(a, b, dims=NN):
    return lax.dot_general(a, b, dims, preferred_element_type=F32)


def pieces(value, count):
    out = []
    for _ in range(count):
        part = value.astype(BF16)
        out.append(part)
        value = value - part.astype(F32)
    return out


def total(ref, count):
    value = ref[0]
    for i in range(1, count):
        value = value + ref[i]
    return value


def kernel(
    acts, cot, base, at, b, mag,
    gx_out, gaf, gb_out, gm_out,
    w, actsf, gf, scaled, bf, ah, ar, mybase,
    sqx, sqz, ns, tbp, tbi, ctp, cti, ctx, ctz, ctc,
    tpp, tpi, tps, tpzi, tpg, mox, moz, moq, gxb, lowo, momt, wts, inr,
    ssem, rsem, lsem,
):
    p = lax.axis_index("dp")
    f = lax.axis_index("fsdp")
    y = lax.axis_index("col")
    x = lax.rem(f, NX)
    z = lax.div(f, NX)
    q = 2 * y + p

    def at_xz(nx, nz):
        return (p, nz * NX + nx, y)

    def at_q(nq):
        return (lax.rem(nq, 2), f, lax.div(nq, 2))

    xpeer = lambda d: at_xz(lax.rem(x + d, NX), z)
    zpeer = lambda d: at_xz(x, lax.rem(z + d, NZ))
    qpeer = lambda d: at_q(lax.rem(q + d, NQ))
    ypeer = lambda d: (p, f, lax.rem(y + d, NY))
    core = (1 - p, f, y)
    h = lax.rem(lax.div(x + 1, 2), 2)
    partner = (p, f + 1 - 2 * lax.rem(x, 2), y)
    cross = (1 - p, f + 1 - 2 * lax.rem(x, 2), y)
    across_x = at_xz(NX - 1 - x, z)
    own_slot = lax.div(x, 2)
    slot_of = lambda jj: lax.rem(own_slot + jj, 2)

    def turned(half, layer):
        return lax.rem(half + lax.rem(layer, 2) * (NY - 2 * half), NY)

    def shift(c, layer):
        k, half = lax.rem(c, 2), turned(lax.div(c, 2), layer)
        return lax.rem((1 - k) * half + k * (4 + (4 - half) * jnp.minimum(half, 1)), NZ)

    def chunk_at(position):
        step = lax.rem(position - q + NZ, NZ)
        far = lax.div(step, 4)
        c = (1 - far) * 2 * step + far * lax.rem(17 - 2 * step, NZ)
        return 2 * turned(lax.div(c, 2), q) + lax.rem(c, 2)

    target = (lax.rem(z, 2), lax.rem(z + shift(q, z), NZ) * NX + x, lax.div(z, 2))
    own = chunk_at(z)
    source = (lax.rem(own, 2), q * NX + x, lax.div(own, 2))
    fixed = jnp.logical_and(own == q, z == q)

    counts = {"send": 0, "recv": 0, "local": 0}
    limits = {"send": SENDS, "recv": RECVS, "local": LOCALS}
    finals = []

    def sems(kind, n=1):
        counts[kind] += n
        assert counts[kind] <= limits[kind]
        return counts[kind] - n

    def copy(src, dst, send, recv, dev):
        return pltpu.make_async_remote_copy(
            src_ref=src, dst_ref=dst, send_sem=ssem.at[send], recv_sem=rsem.at[recv],
            device_id=dev, device_id_type=MESH,
        )

    def arrived(ref, recv):
        copy(ref, ref, 0, recv, core).wait_recv()

    def sent(ref, send):
        finals.append(lambda: copy(ref, ref, send, 0, core).wait_send())

    def each(lo, hi, body):
        def step(i, carry):
            body(i)
            return carry

        lax.fori_loop(lo, hi, step, 0)

    class Ring:
        def __init__(self, n, me, peer, dst):
            self.n, self.me, self.peer, self.dst = n, me, peer, dst
            self.send, self.recv = sems("send"), sems("recv")

        def start(self, src):
            def one(d):
                block = src(lax.rem(self.me + d, self.n))
                copy(block, self.dst.at[self.me], self.send, self.recv, self.peer(d)).start()

            each(1, self.n, one)
            sent(self.dst.at[pl.ds(0, self.n - 1)], self.send)

        def wait(self):
            arrived(self.dst.at[pl.ds(0, self.n - 1)], self.recv)

    def tokens_of(core_of, half_of):
        return pl.ds(pl.multiple_of(core_of * 2 * TOK + half_of * TOK, TOK), TOK)

    mine = tokens_of(p, h)
    my_core = pl.ds(pl.multiple_of(p * 2 * TOK, TOK), 2 * TOK)

    def shard(core_of, half_of, j):
        return pl.ds(pl.multiple_of(core_of * HALF + (half_of + j * (3 - 2 * half_of)) * ROWS, 128), ROWS)

    bar = pltpu.get_barrier_semaphore()
    each(1, NX, lambda d: pl.semaphore_signal(bar, inc=1, device_id=xpeer(d), device_id_type=MESH))
    each(1, NZ, lambda d: pl.semaphore_signal(bar, inc=1, device_id=zpeer(d), device_id_type=MESH))
    each(1, NQ, lambda d: pl.semaphore_signal(bar, inc=1, device_id=qpeer(d), device_id_type=MESH))

    pl.semaphore_signal(bar, inc=1, device_id=cross, device_id_type=MESH)

    @pl.when(jnp.logical_not(fixed))
    def _():
        pl.semaphore_signal(bar, inc=1, device_id=source, device_id_type=MESH)

    loads = [
        pltpu.make_async_copy(base.at[p], mybase, lsem.at[sems("local")]),
        pltpu.make_async_copy(at.at[p, :, pl.ds(pl.multiple_of(f * ROWS, ROWS), ROWS)], ar, lsem.at[sems("local")]),
    ]
    for k in range(2):
        for j in range(2):
            cols = pl.ds(pl.multiple_of(q * HALF + (h + j * (3 - 2 * h)) * ROWS, 128), ROWS)
            dst = ah.at[pl.ds(k * RANK, RANK), pl.ds(j * ROWS, ROWS)]
            loads.append(pltpu.make_async_copy(at.at[k, :, cols], dst, lsem.at[sems("local")]))
        loads.append(pltpu.make_async_copy(cot.at[k], gf.at[2 * y + k, mine, :], lsem.at[sems("local")]))
    for j in range(2):
        dst = actsf.at[mine, pl.ds(j * ROWS, ROWS)]
        loads.append(pltpu.make_async_copy(acts.at[:, shard(p, h, j)], dst, lsem.at[sems("local")]))
    for load in loads:
        load.start()

    @pl.when(jnp.logical_not(fixed))
    def _():
        pl.semaphore_wait(bar, NX + NZ + NQ - 1)

    @pl.when(fixed)
    def _():
        pl.semaphore_wait(bar, NX + NZ + NQ - 2)

    PARTS = ((0, CUT), (CUT, ROWS))
    s_swap, r_swap = sems("send"), sems("recv", 2)

    def swap_copy(i):
        lo, hi = PARTS[i]
        return copy(base.at[p, pl.ds(lo, hi - lo), :], w.at[q, own_slot, pl.ds(lo, hi - lo), :], s_swap, r_swap + i, target)

    @pl.when(jnp.logical_not(fixed))
    def _():
        swap_copy(1).start()
        swap_copy(0).start()

    def wait_swap(i):
        lo, hi = PARTS[i]

        @pl.when(jnp.logical_not(fixed))
        def _():
            arrived(w.at[own, own_slot, pl.ds(lo, hi - lo), :], r_swap + i)

        @pl.when(fixed)
        def _():
            w[own, own_slot, lo:hi, :] = mybase[lo:hi, :]

    def final_swap():
        @pl.when(jnp.logical_not(fixed))
        def _():
            copy(mybase, mybase, s_swap, 0, target).wait_send()

    finals.append(final_swap)
    r_sqx = Ring(NX, x, xpeer, sqx)
    r_sqz = Ring(NZ, z, zpeer, sqz)
    r_ns = Ring(NQ, q, qpeer, ns)
    for load in loads:
        load.wait()
    composed = mybase[...].astype(F32) + dot(ar[...], b[p], TN)
    sqx[x] = jnp.broadcast_to(jnp.sum(composed * composed, axis=0, keepdims=True), (8, COLS))
    across = functools.reduce(lambda u, v: u + v, [dot(ar[...], c) for c in pieces(composed, 3)])

    r_sqx.start(lambda _: sqx.at[x])

    s_gotx, s_goty, s_gotc = sems("send"), sems("send"), sems("send")
    r_gotx, r_goty, r_gotc = sems("recv"), sems("recv", 6), sems("recv")
    parts_of_pair = (mine, tokens_of(p, 1 - h))
    two = gf.at[0, my_core, :]
    def cot_y(i, source=None):
        for turn in range(2):
            for k in range(2):
                there = gf.at[2 * y + k, parts_of_pair[i], :]
                src = there if source is None else source.at[k]
                copy(src, there, s_goty, r_goty + 3 * i + turn, ypeer(1 if turn == 0 else NY - 1)).start()

    def cot_forward(i):
        for turn in range(2):
            arrived(two, r_goty + 3 * i + turn)
            yy = lax.rem(y + (NY - 1 if turn == 0 else 1), NY)
            here = gf.at[2 * yy + turn, parts_of_pair[i], :]
            copy(here, here, s_goty, r_goty + 3 * i + 2, ypeer(1 if turn == 0 else NY - 1)).start()

    def cot_core(d):
        for k in range(2):
            here = gf.at[2 * lax.rem(y - d + NY, NY) + k, my_core, :]
            copy(here, here, s_gotc, r_gotc, core).start()

    cot_y(0, cot)
    for k in range(2):
        copy(cot.at[k], gf.at[2 * y + k, mine, :], s_gotx, r_gotx, partner).start()
    sent(two, s_gotx)

    sent(gf.at[pl.ds(0, NY - 1)], s_goty)
    sent(gf.at[pl.ds(0, NY)], s_gotc)

    def cot_start():
        arrived(two, r_gotx)
        cot_y(1)
        cot_core(0)

    def cot_relay():
        cot_forward(1)
        cot_core(1)
        cot_core(3)

    def cot_relay_last():
        for i in range(2):
            arrived(two, r_goty + 3 * i + 2)
        cot_core(2)

    def cot_wait():
        arrived(gf.at[pl.ds(0, NY)], r_gotc)

    s_acts, r_acts = sems("send"), sems("recv")

    def acts_start(j):
        for core_of, half_of, dev in ((p, 1 - h, partner), (1 - p, 1 - h, cross), (1 - p, h, core)):
            dst = actsf.at[mine, pl.ds(j * ROWS, ROWS)]
            copy(acts.at[:, shard(core_of, half_of, j)], dst, s_acts, r_acts, dev).start()

    acts_start(0)
    sent(actsf.at[pl.ds(0, 3 * TOK), :], s_acts)

    def acts_wait():
        arrived(actsf.at[pl.ds(0, 3 * TOK), :], r_acts)

    r_b = Ring(NY, y, ypeer, bf)
    bf[y] = b[...]
    r_b.start(lambda i: bf.at[y])

    s_ax, s_az, s_bz, s_bx = sems("send"), sems("send"), sems("send"), sems("send")
    r_ax, r_az, r_bz = sems("recv"), sems("recv", 2 * 8), sems("recv", 8)
    r_bx, r_bx4 = sems("recv", 7), sems("recv")
    b_lo, b_n = CUT, ROWS - CUT
    b_half = b_n // 2

    def ring_rows(part, way, s):
        lo, hi = PARTS[part]
        if s < 3:
            return lo, hi - lo
        half = (hi - lo) // 2
        return lo + way * half, half

    def origin(way, s):
        return chunk_at(lax.rem(z - s + NZ, NZ) if way == 0 else lax.rem(z + s, NZ))

    def z_sem(part, j, way, s):
        return (r_az + (j * 2 + way) * 4 + s) if part == 0 else (r_bz + way * 4 + s)

    def z_start(part, j, way, s):
        lo, n = ring_rows(part, way, s)
        here = w.at[origin(way, s), slot_of(j), pl.ds(lo, n), :]
        send = s_az if part == 0 else s_bz
        copy(here, here, send, z_sem(part, j, way, s), zpeer(1 if way == 0 else NZ - 1)).start()

    def z_arrival(part, j, way, s):
        lo, n = ring_rows(part, way, s)
        arrived(w.at[origin(way, s + 1), slot_of(j), pl.ds(lo, n), :], z_sem(part, j, way, s))

    sent(w.at[pl.ds(0, 7), :, pl.ds(0, CUT), :], s_az)
    sent(w.at[pl.ds(0, 7), 0, pl.ds(b_lo, b_n), :], s_bz)
    sent(w.at[pl.ds(0, 4), :, pl.ds(b_lo, b_n), :], s_bx)
    sent(w.at[0, 0, pl.ds(0, CUT), :], s_ax)

    def bx_sem(way, s):
        return r_bx + (0 if s == 0 else 1 + way * 3 + s - 1)

    def bx_start(way, s):
        here = w.at[origin(way, s), own_slot, pl.ds(b_lo, b_n), :]
        copy(here, here, s_bx, bx_sem(way, s), across_x).start()

    def bx_wait(way, s):
        arrived(w.at[origin(way, s), slot_of(1), pl.ds(b_lo, b_n), :], bx_sem(way, s))

    def bx4_start(way):
        here = w.at[origin(way, 4), own_slot, pl.ds(b_lo + way * b_half, b_half), :]
        copy(here, here, s_bx, r_bx4, across_x).start()

    def bx4_wait():
        arrived(w.at[origin(0, 4), slot_of(1), pl.ds(b_lo, b_n), :], r_bx4)

    r_sqx.wait()
    sqz[z] = total(sqx, NX)
    r_sqz.start(lambda _: sqz.at[z])
    cot_start()
    wait_swap(1)
    for way in range(2):
        z_start(1, 0, way, 0)
    wait_swap(0)
    here_a = w.at[own, own_slot, pl.ds(0, CUT), :]
    copy(here_a, here_a, s_ax, r_ax, across_x).start()
    for way in range(2):
        z_start(0, 0, way, 0)
    bx_start(0, 0)
    acts_start(1)
    cot_forward(0)
    arrived(w.at[own, slot_of(1), pl.ds(0, CUT), :], r_ax)
    for way in range(2):
        z_start(0, 1, way, 0)
    r_sqz.wait()
    norms = jnp.sqrt(total(sqz, NZ)[0:1])
    ns[q, 0:1] = norms
    ns[q, 1:2] = mag[pl.ds(p, 1), :] / norms
    r_ns.start(lambda _: ns.at[q])
    def ring_b(s):
        for way in range(2):
            z_arrival(1, 0, way, s - 1)
            if s < 4:
                z_start(1, 0, way, s)
                bx_start(way, s)
            else:
                bx4_start(way)

    def ring_a(j, s):
        for way in range(2):
            z_arrival(0, j, way, s - 1)
            if s < 4:
                z_start(0, j, way, s)

    def forward(zi):
        weight = w[zi].reshape(WORK, COLS)
        acc = jnp.zeros((8, COLS), F32)
        for lo in range(0, PAIR, TILE):
            out = dot(actsf[lo : lo + TILE, :], weight)
            acc = acc + jnp.sum((out * gf[zi, lo : lo + TILE, :].astype(F32)).reshape(TILE // 8, 8, COLS), axis=0)
        momt[pl.ds(zi, 1), :] = jnp.sum(acc, axis=0, keepdims=True)

    r_tb = Ring(NQ, q, qpeer, tbi)
    r_ctz = Ring(NZ, z, zpeer, cti)
    r_ctx = Ring(NX, x, xpeer, ctx)
    r_ctg = Ring(NZ, z, zpeer, ctz)
    s_tpx, r_tpx = sems("send"), sems("recv")
    r_tpz = Ring(NZ, z, zpeer, tpzi)
    r_tpg = Ring(NZ, z, zpeer, tpg)

    def send_token_b():
        low_in = dot(ah[...], actsf[...], NT)
        for k in range(2):
            parts = jnp.concatenate(pieces(low_in[k * RANK : (k + 1) * RANK], 3), axis=0)
            for yy in range(NY):
                t = dot(parts, gf[2 * yy + k])
                tbp[2 * yy + k] = t[0:RANK] + t[RANK : 2 * RANK] + t[2 * RANK :]
        tbi[q] = tbp[q]
        r_tb.start(lambda i: tbp.at[i])

    def send_tokens():
        r_ns.wait()
        low = []
        for lo in range(0, PAIR, TILE):
            rows = slice(lo, lo + TILE)
            halves = []
            for k in range(2):
                acc = None
                for yy in range(NY):
                    i = 2 * yy + k
                    s = (gf[i, rows, :].astype(F32) * ns[i, 1:2]).astype(BF16)
                    scaled[i, rows, :] = s
                    t = dot(s, bf[yy, k], NT)
                    acc = t if acc is None else acc + t
                halves.append(acc)
            low.append(jnp.concatenate(halves, axis=1))
        lowf = jnp.concatenate(low, axis=0)
        lowo[...] = lowf.astype(BF16)
        lowt = lowf.T.astype(BF16)
        for j in range(2):
            tpp[j] = dot(lowt, actsf[:, j * ROWS : (j + 1) * ROWS])
        copy(tpp.at[slot_of(1)], tpi, s_tpx, r_tpx, across_x).start()
        sent(tpi, s_tpx)

    def sum_tokens_x():
        arrived(tpi, r_tpx)
        tps[...] = (tpp[own_slot] + tpi[...]).reshape(NZ, 8, ROWS)
        tpzi[z] = tps[z]
        r_tpz.start(lambda i: tps.at[i])

    def sum_tokens_z():
        r_tpz.wait()
        tpg[z] = total(tpzi, NZ)
        r_tpg.start(lambda _: tpg.at[z])

    def sum_products_q():
        r_tb.wait()
        token_b = total(tbi, NQ)
        for g in range(NZ):
            ctp[g, 0:4] = across[4 * g : 4 * g + 4]
            ctp[g, 4:8] = token_b[4 * g : 4 * g + 4]
        cti[z] = ctp[z]
        r_ctz.start(lambda i: ctp.at[i])

    def sum_products_z():
        r_ctz.wait()
        ctx[x] = total(cti, NZ)
        r_ctx.start(lambda _: ctx.at[x])

    def sum_products_x():
        r_ctx.wait()
        ctz[z] = total(ctx, NX)
        r_ctg.start(lambda _: ctz.at[z])

    def column_sums(way, s):
        bx_wait(way, s)
        forward(origin(way, s))

    ring_b(1)
    ring_a(0, 1)
    cot_relay()
    ring_a(1, 1)
    ring_b(2)
    ring_a(0, 2)
    r_b.wait()
    cot_relay_last()
    ring_a(1, 2)
    ring_b(3)
    cot_wait()
    acts_wait()
    send_tokens()
    send_token_b()
    ring_a(0, 3)
    ring_a(1, 3)
    column_sums(0, 0)
    ring_b(4)
    column_sums(0, 1)
    column_sums(1, 1)
    ring_a(0, 4)
    column_sums(0, 2)
    column_sums(1, 2)
    ring_a(1, 4)
    column_sums(0, 3)
    column_sums(1, 3)
    sum_tokens_x()
    bx4_wait()
    forward(origin(0, 4))

    r_mox = Ring(NX, x, xpeer, mox)
    r_moz = Ring(NZ, z, zpeer, moz)
    r_moq = Ring(NQ, q, qpeer, moq)
    extra = []
    for i in range(NQ):
        extra.append(jnp.sum(tbp[i] * bf[i // 2, i % 2].astype(F32), axis=0, keepdims=True))
    mox[x] = momt[...] + jnp.concatenate(extra, axis=0)
    r_mox.start(lambda _: mox.at[x])

    s_gx, r_gx = sems("send"), sems("recv")
    l_gx = sems("local")

    def backward(j):
        cols = slice(j * ROWS, (j + 1) * ROWS)
        acc = dot(lowo[...], ah[:, cols])
        for zi in range(NZ):
            acc = acc + dot(scaled[zi], w[zi, j], NT)
        gxb[:, cols] = acc.astype(BF16)

    def gx_start(j):
        there = gx_out.at[:, shard(p, h, j)]
        part = pl.ds(j * ROWS, ROWS)
        for core_of, half_of, dev in ((p, 1 - h, partner), (1 - p, 1 - h, cross), (1 - p, h, core)):
            copy(gxb.at[tokens_of(core_of, half_of), part], there, s_gx, r_gx, dev).start()
        pltpu.make_async_copy(gxb.at[mine, part], there, lsem.at[l_gx]).start()

    backward(0)
    gx_start(0)
    sum_products_q()
    r_mox.wait()
    moz[z] = total(mox, NX)
    r_moz.start(lambda _: moz.at[z])
    backward(1)
    sum_tokens_z()
    sum_products_z()
    gx_start(1)
    r_moz.wait()
    moq[q] = total(moz, NZ)
    r_moq.start(lambda _: moq.at[q])
    r_moq.wait()
    moment = total(moq, NQ)
    norm_all = jnp.concatenate([ns[i, 0:1] for i in range(NQ)], axis=0)
    scal_all = jnp.concatenate([ns[i, 1:2] for i in range(NQ)], axis=0)
    grad_mag = moment / norm_all
    factor = scal_all * grad_mag / norm_all
    momt[...] = grad_mag

    for k in range(2):
        inner = None
        for yy in range(NY):
            i = 2 * yy + k
            two = jnp.concatenate(pieces(bf[yy, k].astype(F32) * factor[i : i + 1], 2), axis=0)
            wts[i] = two
            t = dot(two, bf[yy, k], NT)
            inner = t if inner is None else inner + t
        inr[k] = jnp.concatenate(pieces(inner[0:RANK] + inner[RANK:], 2), axis=0)

    s_ga, s_gac = sems("send"), sems("send")
    r_first, r_second, r_gac = sems("recv", NX), sems("recv", 3 * NX), sems("recv")

    def ga_block(k, a, b):
        dy, dx = (a, b) if k == 0 else (b, a)
        block = gaf.at[2 * lax.rem(y - dy + NY, NY) + p, lax.rem(x - dx + NX, NX)]
        return block.at[pl.ds(k * RANK, RANK), :]

    def ga_peer(k, axis, d):
        return ypeer(d) if k == axis else xpeer(d)

    def ga_core(here):
        copy(here, here, s_gac, r_gac, core).start()

    def ga_second(k, a):
        here = ga_block(k, a, 0)
        for turn in range(2):
            sem = r_second + 3 * a + turn
            copy(here, here, s_ga, sem, ga_peer(k, 1, 1 if turn == 0 else 3)).start()
        ga_core(here)

    def ga_start(k):
        here = ga_block(k, 0, 0)
        for d in (1, 3, 2):
            copy(here, here, s_ga, r_first + d, ga_peer(k, 0, d)).start()
        ga_second(k, 0)

    whole = gaf.at[0, 0]

    def ga_first(a):
        arrived(whole, r_first + a)
        for k in range(2):
            ga_second(k, a)

    def ga_forward(a):
        for turn in range(2):
            arrived(whole, r_second + 3 * a + turn)
            for k in range(2):
                here = ga_block(k, a, 1 if turn == 0 else 3)
                if (a in (0, 2)) == (turn == 0):
                    sem = r_second + 3 * a + 2
                    copy(here, here, s_ga, sem, ga_peer(k, 1, 1 if turn == 0 else 3)).start()
                ga_core(here)

    def ga_last(a):
        arrived(whole, r_second + 3 * a + 2)
        for k in range(2):
            ga_core(ga_block(k, a, 2))

    r_tpg.wait()
    tokens = tpg[...].reshape(2 * RANK, ROWS)
    span = pl.ds(pl.multiple_of(own_slot * ROWS, 128), ROWS)
    for k in range(2):
        acc = dot(inr[k], ah[k * RANK : (k + 1) * RANK, span])
        for yy in range(NY):
            acc = acc + dot(wts[2 * yy + k], w[2 * yy + k, own_slot], NT)
        rows = slice(k * RANK, (k + 1) * RANK)
        gaf[q, x, rows, :] = (tokens[rows] - (acc[0:RANK] + acc[RANK:])).astype(BF16)
        ga_start(k)

    sum_products_x()
    ga_first(1)
    ga_first(3)
    ga_forward(0)
    ga_first(2)
    r_ctg.wait()
    ctc[p] = ctz[...]
    s_ctc, r_ctc = sems("send"), sems("recv")
    copy(ctc.at[p], ctc.at[p], s_ctc, r_ctc, core).start()
    sent(ctc.at[p], s_ctc)
    ga_forward(1)
    ga_forward(3)
    ga_forward(2)
    for a in (0, 1, 3, 2):
        ga_last(a)
    arrived(ctc.at[1 - p], r_ctc)
    for k in range(2):
        i = 2 * y + k
        norm_k = ns[i, 0:1]
        scal_k = ns[i, 1:2]
        gm_k = momt[pl.ds(i, 1), :]
        gm_out[k : k + 1] = gm_k
        ratio = gm_k / norm_k
        for g in range(NZ):
            gb_out[k, 4 * g : 4 * g + 4] = scal_k * (ctc[k, g, 4:8] - ctc[k, g, 0:4] * ratio)

    arrived(gaf.at[pl.ds(0, NY)], r_gac)
    arrived(gxb.at[pl.ds(0, 3 * TOK), :], r_gx)
    sent(gxb.at[pl.ds(0, 3 * TOK), :], s_gx)
    pltpu.make_async_copy(gxb.at[mine, :], gxb.at[mine, :], lsem.at[l_gx]).wait()
    sent(gaf.at[pl.ds(0, 5), pl.ds(0, 3)], s_ga)
    sent(gaf.at[pl.ds(0, NY)], s_gac)
    assert counts == limits, counts
    for final in finals:
        final()


SENDS, RECVS, LOCALS = 27, 77, 11


def finish(gx, ga, gb, gm):
    def widen(gx_in, ga_in, gb_in, gm_in, gx_to, ga_to, gb_to, gm_to, full, gx_sem, ga_sem):
        pltpu.make_async_copy(gx_in, gx_to, gx_sem).start()
        gb_to[...] = gb_in[...]
        gm_to[...] = gm_in[...]
        for i in range(NQ):
            for xx in range(NX):
                for k in range(2):
                    block = ga_in[i, xx, k * RANK : (k + 1) * RANK, :]
                    full[i, k, :, xx * ROWS : (xx + 1) * ROWS] = block.astype(F32)
            pltpu.make_async_copy(full.at[i], ga_to.at[:, :, pl.ds(i * HALF, HALF)], ga_sem).start()
        pltpu.make_async_copy(full, full, ga_sem).wait()
        pltpu.make_async_copy(gx_in, gx_in, gx_sem).wait()

    vm = pl.BlockSpec(memory_space=pltpu.VMEM)
    hbm = pl.BlockSpec(memory_space=pl.ANY)
    return pl.pallas_call(
        widen,
        out_shape=(
            jax.ShapeDtypeStruct(gx.shape, BF16),
            jax.ShapeDtypeStruct((2, RANK, NQ * HALF), F32),
            jax.ShapeDtypeStruct(gb.shape, F32),
            jax.ShapeDtypeStruct(gm.shape, F32),
        ),
        in_specs=[vm, vm, vm, vm],
        out_specs=(hbm, hbm, vm, vm),
        scratch_shapes=[
            pltpu.VMEM((NQ, 2, RANK, HALF), F32),
            pltpu.SemaphoreType.DMA,
            pltpu.SemaphoreType.DMA,
        ],
        compiler_params=pltpu.CompilerParams(vmem_limit_bytes=16 * 2**20),
    )(gx, ga, gb, gm)


def on_device(acts, cot, base, adapter_a, adapter_b, magnitude):
    at = jnp.swapaxes(adapter_a, 1, 2)
    vm = pl.BlockSpec(memory_space=pltpu.VMEM)
    hbm = pl.BlockSpec(memory_space=pl.ANY)
    scratch = [
        ((NZ, 2, ROWS, COLS), BF16),
        ((PAIR, WORK), BF16),
        ((NQ, PAIR, COLS), BF16),
        ((NQ, PAIR, COLS), BF16),
        ((NY, 2, RANK, COLS), BF16),
        ((2 * RANK, WORK), BF16),
        ((RANK, ROWS), BF16),
        ((ROWS, COLS), BF16),
        ((NX, 8, COLS), F32),
        ((NZ, 8, COLS), F32),
        ((NQ, 8, COLS), F32),
        ((NQ, RANK, COLS), F32),
        ((NQ, RANK, COLS), F32),
        ((NZ, 8, COLS), F32),
        ((NZ, 8, COLS), F32),
        ((NX, 8, COLS), F32),
        ((NZ, 8, COLS), F32),
        ((2, NZ, 8, COLS), F32),
        ((2, 2 * RANK, ROWS), F32),
        ((2 * RANK, ROWS), F32),
        ((NZ, 8, ROWS), F32),
        ((NZ, 8, ROWS), F32),
        ((NZ, 8, ROWS), F32),
        ((NX, 8, COLS), F32),
        ((NZ, 8, COLS), F32),
        ((NQ, 8, COLS), F32),
        ((PAIR, WORK), BF16),
        ((PAIR, 2 * RANK), BF16),
        ((NQ, COLS), F32),
        ((NQ, 2 * RANK, COLS), BF16),
        ((2, 2 * RANK, RANK), BF16),
    ]
    gx, ga, gb, gm = pl.pallas_call(
        kernel,
        out_shape=(
            pltpu.VMEM((TOK, FEAT), BF16),
            pltpu.VMEM((NQ, NX, 2 * RANK, ROWS), BF16),
            pltpu.VMEM((2, RANK, COLS), F32),
            pltpu.VMEM((2, COLS), F32),
        ),
        in_specs=[hbm, hbm, hbm, hbm, vm, vm],
        out_specs=(vm, vm, vm, vm),
        scratch_shapes=[pltpu.VMEM(shape, dtype) for shape, dtype in scratch]
        + [pltpu.SemaphoreType.DMA((n,)) for n in (SENDS, RECVS, LOCALS)],
        compiler_params=pltpu.CompilerParams(
            collective_id=0, has_side_effects=True, vmem_limit_bytes=58 * 2**20
        ),
        cost_estimate=pl.CostEstimate(flops=5 * 10**9, bytes_accessed=8 * 10**6, transcendentals=0),
    )(acts, cot, base, at, adapter_b, magnitude)
    gx, ga, gb, gm = finish(gx, ga, gb, gm)
    return gx, jnp.swapaxes(ga, 1, 2), gb, gm


def solution(mesh):
    in_specs = (
        P(("dp", "fsdp"), "col"),
        P(None, ("dp", "fsdp"), "col"),
        P(None, "fsdp", "col"),
        P(),
        P(None, None, "col"),
        P(None, "col"),
    )
    out_specs = (P(("dp", "fsdp"), "col"), P(), P(None, None, "col"), P(None, "col"))
    return jax.shard_map(
        on_device, mesh=mesh, in_specs=in_specs, out_specs=out_specs, check_vma=False
    )
```

```python
import functools

import jax
import jax.numpy as jnp
from jax import lax
from jax.experimental import pallas as pl
from jax.experimental.pallas import tpu as pltpu
from jax.sharding import PartitionSpec as P

MESH = pl.DeviceIdType.MESH
F32 = jnp.float32
BF16 = jnp.bfloat16

NX, NZ, NY = 4, 8, 4
NQ = 2 * NY

TOK = 192
PAIR = 4 * TOK
FEAT = 3072
HALF = FEAT // 2
COLS = 256
ROWS = 384
WORK = 2 * ROWS
RANK = 32
TILE = 128
CUT = 192

NT = (((1,), (1,)), ((), ()))
TN = (((0,), (0,)), ((), ()))
NN = (((1,), (0,)), ((), ()))


def dot(a, b, dims=NN):
    return lax.dot_general(a, b, dims, preferred_element_type=F32)


def pieces(value, count):
    out = []
    for _ in range(count):
        part = value.astype(BF16)
        out.append(part)
        value = value - part.astype(F32)
    return out


def total(ref, count):
    value = ref[0]
    for i in range(1, count):
        value = value + ref[i]
    return value


def kernel(
    acts, cot, base, at, b, mag,
    gx_out, gaf, gb_out, gm_out,
    w, actsf, gf, scaled, bf, ah, ar, mybase,
    sqx, sqz, ns, tbp, tbi, ctp, cti, ctx, ctz, ctc,
    tpp, tpi, tps, tpzi, tpg, mox, moz, moq, gxb, lowo, momt, wts, inr,
    ssem, rsem, lsem,
):
    p = lax.axis_index("dp")
    f = lax.axis_index("fsdp")
    y = lax.axis_index("col")
    x = lax.rem(f, NX)
    z = lax.div(f, NX)
    q = 2 * y + p

    def at_xz(nx, nz):
        return (p, nz * NX + nx, y)

    def at_q(nq):
        return (lax.rem(nq, 2), f, lax.div(nq, 2))

    xpeer = lambda d: at_xz(lax.rem(x + d, NX), z)
    zpeer = lambda d: at_xz(x, lax.rem(z + d, NZ))
    qpeer = lambda d: at_q(lax.rem(q + d, NQ))
    ypeer = lambda d: (p, f, lax.rem(y + d, NY))
    core = (1 - p, f, y)
    h = lax.rem(lax.div(x + 1, 2), 2)
    partner = (p, f + 1 - 2 * lax.rem(x, 2), y)
    cross = (1 - p, f + 1 - 2 * lax.rem(x, 2), y)
    across_x = at_xz(NX - 1 - x, z)
    own_slot = lax.div(x, 2)
    slot_of = lambda jj: lax.rem(own_slot + jj, 2)

    def turned(half, layer):
        return lax.rem(half + lax.rem(layer, 2) * (NY - 2 * half), NY)

    def shift(c, layer):
        k, half = lax.rem(c, 2), turned(lax.div(c, 2), layer)
        return lax.rem((1 - k) * half + k * (4 + (4 - half) * jnp.minimum(half, 1)), NZ)

    def chunk_at(position):
        step = lax.rem(position - q + NZ, NZ)
        far = lax.div(step, 4)
        c = (1 - far) * 2 * step + far * lax.rem(17 - 2 * step, NZ)
        return 2 * turned(lax.div(c, 2), q) + lax.rem(c, 2)

    target = (lax.rem(z, 2), lax.rem(z + shift(q, z), NZ) * NX + x, lax.div(z, 2))
    own = chunk_at(z)
    source = (lax.rem(own, 2), q * NX + x, lax.div(own, 2))
    fixed = jnp.logical_and(own == q, z == q)

    counts = {"send": 0, "recv": 0, "local": 0}
    limits = {"send": SENDS, "recv": RECVS, "local": LOCALS}
    finals = []

    def sems(kind, n=1):
        counts[kind] += n
        assert counts[kind] <= limits[kind]
        return counts[kind] - n

    def copy(src, dst, send, recv, dev):
        return pltpu.make_async_remote_copy(
            src_ref=src, dst_ref=dst, send_sem=ssem.at[send], recv_sem=rsem.at[recv],
            device_id=dev, device_id_type=MESH,
        )

    def arrived(ref, recv):
        copy(ref, ref, 0, recv, core).wait_recv()

    def sent(ref, send):
        finals.append(lambda: copy(ref, ref, send, 0, core).wait_send())

    def each(lo, hi, body):
        def step(i, carry):
            body(i)
            return carry

        lax.fori_loop(lo, hi, step, 0)

    class Ring:
        def __init__(self, n, me, peer, dst):
            self.n, self.me, self.peer, self.dst = n, me, peer, dst
            self.send, self.recv = sems("send"), sems("recv")

        def start(self, src):
            def one(d):
                block = src(lax.rem(self.me + d, self.n))
                copy(block, self.dst.at[self.me], self.send, self.recv, self.peer(d)).start()

            each(1, self.n, one)
            sent(self.dst.at[pl.ds(0, self.n - 1)], self.send)

        def wait(self):
            arrived(self.dst.at[pl.ds(0, self.n - 1)], self.recv)

    def tokens_of(core_of, half_of):
        return pl.ds(pl.multiple_of(core_of * 2 * TOK + half_of * TOK, TOK), TOK)

    mine = tokens_of(p, h)
    my_core = pl.ds(pl.multiple_of(p * 2 * TOK, TOK), 2 * TOK)

    def shard(core_of, half_of, j):
        return pl.ds(pl.multiple_of(core_of * HALF + (half_of + j * (3 - 2 * half_of)) * ROWS, 128), ROWS)

    bar = pltpu.get_barrier_semaphore()
    each(1, NX, lambda d: pl.semaphore_signal(bar, inc=1, device_id=xpeer(d), device_id_type=MESH))
    each(1, NZ, lambda d: pl.semaphore_signal(bar, inc=1, device_id=zpeer(d), device_id_type=MESH))
    each(1, NQ, lambda d: pl.semaphore_signal(bar, inc=1, device_id=qpeer(d), device_id_type=MESH))

    pl.semaphore_signal(bar, inc=1, device_id=cross, device_id_type=MESH)

    @pl.when(jnp.logical_not(fixed))
    def _():
        pl.semaphore_signal(bar, inc=1, device_id=source, device_id_type=MESH)

    loads = [
        pltpu.make_async_copy(base.at[p], mybase, lsem.at[sems("local")]),
        pltpu.make_async_copy(at.at[p, :, pl.ds(pl.multiple_of(f * ROWS, ROWS), ROWS)], ar, lsem.at[sems("local")]),
    ]
    for k in range(2):
        for j in range(2):
            cols = pl.ds(pl.multiple_of(q * HALF + (h + j * (3 - 2 * h)) * ROWS, 128), ROWS)
            dst = ah.at[pl.ds(k * RANK, RANK), pl.ds(j * ROWS, ROWS)]
            loads.append(pltpu.make_async_copy(at.at[k, :, cols], dst, lsem.at[sems("local")]))
        loads.append(pltpu.make_async_copy(cot.at[k], gf.at[2 * y + k, mine, :], lsem.at[sems("local")]))
    for j in range(2):
        dst = actsf.at[mine, pl.ds(j * ROWS, ROWS)]
        loads.append(pltpu.make_async_copy(acts.at[:, shard(p, h, j)], dst, lsem.at[sems("local")]))
    for load in loads:
        load.start()

    @pl.when(jnp.logical_not(fixed))
    def _():
        pl.semaphore_wait(bar, NX + NZ + NQ - 1)

    @pl.when(fixed)
    def _():
        pl.semaphore_wait(bar, NX + NZ + NQ - 2)

    PARTS = ((0, CUT), (CUT, ROWS))
    s_swap, r_swap = sems("send"), sems("recv", 2)

    def swap_copy(i):
        lo, hi = PARTS[i]
        return copy(base.at[p, pl.ds(lo, hi - lo), :], w.at[q, own_slot, pl.ds(lo, hi - lo), :], s_swap, r_swap + i, target)

    @pl.when(jnp.logical_not(fixed))
    def _():
        swap_copy(1).start()
        swap_copy(0).start()

    def wait_swap(i):
        lo, hi = PARTS[i]

        @pl.when(jnp.logical_not(fixed))
        def _():
            arrived(w.at[own, own_slot, pl.ds(lo, hi - lo), :], r_swap + i)

        @pl.when(fixed)
        def _():
            w[own, own_slot, lo:hi, :] = mybase[lo:hi, :]

    def final_swap():
        @pl.when(jnp.logical_not(fixed))
        def _():
            copy(mybase, mybase, s_swap, 0, target).wait_send()

    finals.append(final_swap)
    r_sqx = Ring(NX, x, xpeer, sqx)
    r_sqz = Ring(NZ, z, zpeer, sqz)
    r_ns = Ring(NQ, q, qpeer, ns)
    for load in loads:
        load.wait()
    composed = mybase[...].astype(F32) + dot(ar[...], b[p], TN)
    sqx[x] = jnp.broadcast_to(jnp.sum(composed * composed, axis=0, keepdims=True), (8, COLS))
    across = functools.reduce(lambda u, v: u + v, [dot(ar[...], c) for c in pieces(composed, 3)])

    r_sqx.start(lambda _: sqx.at[x])

    s_gotx, s_goty, s_gotc = sems("send"), sems("send"), sems("send")
    r_gotx, r_goty, r_gotc = sems("recv"), sems("recv", 6), sems("recv")
    parts_of_pair = (mine, tokens_of(p, 1 - h))
    two = gf.at[0, my_core, :]
    def cot_y(i, source=None):
        for turn in range(2):
            for k in range(2):
                there = gf.at[2 * y + k, parts_of_pair[i], :]
                src = there if source is None else source.at[k]
                copy(src, there, s_goty, r_goty + 3 * i + turn, ypeer(1 if turn == 0 else NY - 1)).start()

    def cot_forward(i):
        for turn in range(2):
            arrived(two, r_goty + 3 * i + turn)
            yy = lax.rem(y + (NY - 1 if turn == 0 else 1), NY)
            here = gf.at[2 * yy + turn, parts_of_pair[i], :]
            copy(here, here, s_goty, r_goty + 3 * i + 2, ypeer(1 if turn == 0 else NY - 1)).start()

    def cot_core(d):
        for k in range(2):
            here = gf.at[2 * lax.rem(y - d + NY, NY) + k, my_core, :]
            copy(here, here, s_gotc, r_gotc, core).start()

    cot_y(0, cot)
    for k in range(2):
        copy(cot.at[k], gf.at[2 * y + k, mine, :], s_gotx, r_gotx, partner).start()
    sent(two, s_gotx)

    sent(gf.at[pl.ds(0, NY - 1)], s_goty)
    sent(gf.at[pl.ds(0, NY)], s_gotc)

    def cot_start():
        arrived(two, r_gotx)
        cot_y(1)
        cot_core(0)

    def cot_relay():
        cot_forward(1)
        cot_core(1)
        cot_core(3)

    def cot_relay_last():
        for i in range(2):
            arrived(two, r_goty + 3 * i + 2)
        cot_core(2)

    def cot_wait():
        arrived(gf.at[pl.ds(0, NY)], r_gotc)

    s_acts, r_acts = sems("send"), sems("recv")

    def acts_start(j):
        for core_of, half_of, dev in ((p, 1 - h, partner), (1 - p, 1 - h, cross), (1 - p, h, core)):
            dst = actsf.at[mine, pl.ds(j * ROWS, ROWS)]
            copy(acts.at[:, shard(core_of, half_of, j)], dst, s_acts, r_acts, dev).start()

    acts_start(0)
    sent(actsf.at[pl.ds(0, 3 * TOK), :], s_acts)

    def acts_wait():
        arrived(actsf.at[pl.ds(0, 3 * TOK), :], r_acts)

    r_b = Ring(NY, y, ypeer, bf)
    bf[y] = b[...]
    r_b.start(lambda i: bf.at[y])

    s_ax, s_az, s_bz, s_bx = sems("send"), sems("send"), sems("send"), sems("send")
    r_ax, r_az, r_bz = sems("recv"), sems("recv", 2 * 8), sems("recv", 8)
    r_bx, r_bx4 = sems("recv", 7), sems("recv")
    b_lo, b_n = CUT, ROWS - CUT
    b_half = b_n // 2

    def ring_rows(part, way, s):
        lo, hi = PARTS[part]
        if s < 3:
            return lo, hi - lo
        half = (hi - lo) // 2
        return lo + way * half, half

    def origin(way, s):
        return chunk_at(lax.rem(z - s + NZ, NZ) if way == 0 else lax.rem(z + s, NZ))

    def z_sem(part, j, way, s):
        return (r_az + (j * 2 + way) * 4 + s) if part == 0 else (r_bz + way * 4 + s)

    def z_start(part, j, way, s):
        lo, n = ring_rows(part, way, s)
        here = w.at[origin(way, s), slot_of(j), pl.ds(lo, n), :]
        send = s_az if part == 0 else s_bz
        copy(here, here, send, z_sem(part, j, way, s), zpeer(1 if way == 0 else NZ - 1)).start()

    def z_arrival(part, j, way, s):
        lo, n = ring_rows(part, way, s)
        arrived(w.at[origin(way, s + 1), slot_of(j), pl.ds(lo, n), :], z_sem(part, j, way, s))

    sent(w.at[pl.ds(0, 7), :, pl.ds(0, CUT), :], s_az)
    sent(w.at[pl.ds(0, 7), 0, pl.ds(b_lo, b_n), :], s_bz)
    sent(w.at[pl.ds(0, 4), :, pl.ds(b_lo, b_n), :], s_bx)
    sent(w.at[0, 0, pl.ds(0, CUT), :], s_ax)

    def bx_sem(way, s):
        return r_bx + (0 if s == 0 else 1 + way * 3 + s - 1)

    def bx_start(way, s):
        here = w.at[origin(way, s), own_slot, pl.ds(b_lo, b_n), :]
        copy(here, here, s_bx, bx_sem(way, s), across_x).start()

    def bx_wait(way, s):
        arrived(w.at[origin(way, s), slot_of(1), pl.ds(b_lo, b_n), :], bx_sem(way, s))

    def bx4_start(way):
        here = w.at[origin(way, 4), own_slot, pl.ds(b_lo + way * b_half, b_half), :]
        copy(here, here, s_bx, r_bx4, across_x).start()

    def bx4_wait():
        arrived(w.at[origin(0, 4), slot_of(1), pl.ds(b_lo, b_n), :], r_bx4)

    r_sqx.wait()
    sqz[z] = total(sqx, NX)
    r_sqz.start(lambda _: sqz.at[z])
    wait_swap(1)
    for way in range(2):
        z_start(1, 0, way, 0)
    wait_swap(0)
    here_a = w.at[own, own_slot, pl.ds(0, CUT), :]
    copy(here_a, here_a, s_ax, r_ax, across_x).start()
    for way in range(2):
        z_start(0, 0, way, 0)
    bx_start(0, 0)
    cot_start()
    acts_start(1)
    cot_forward(0)
    arrived(w.at[own, slot_of(1), pl.ds(0, CUT), :], r_ax)
    for way in range(2):
        z_start(0, 1, way, 0)
    r_sqz.wait()
    norms = jnp.sqrt(total(sqz, NZ)[0:1])
    ns[q, 0:1] = norms
    ns[q, 1:2] = mag[pl.ds(p, 1), :] / norms
    r_ns.start(lambda _: ns.at[q])
    def ring_b(s):
        for way in range(2):
            z_arrival(1, 0, way, s - 1)
            if s < 4:
                z_start(1, 0, way, s)
                bx_start(way, s)
            else:
                bx4_start(way)

    def ring_a(j, s):
        for way in range(2):
            z_arrival(0, j, way, s - 1)
            if s < 4:
                z_start(0, j, way, s)

    def forward(zi):
        weight = w[zi].reshape(WORK, COLS)
        acc = jnp.zeros((8, COLS), F32)
        for lo in range(0, PAIR, TILE):
            out = dot(actsf[lo : lo + TILE, :], weight)
            acc = acc + jnp.sum((out * gf[zi, lo : lo + TILE, :].astype(F32)).reshape(TILE // 8, 8, COLS), axis=0)
        momt[pl.ds(zi, 1), :] = jnp.sum(acc, axis=0, keepdims=True)

    r_tb = Ring(NQ, q, qpeer, tbi)
    r_ctz = Ring(NZ, z, zpeer, cti)
    r_ctx = Ring(NX, x, xpeer, ctx)
    r_ctg = Ring(NZ, z, zpeer, ctz)
    s_tpx, r_tpx = sems("send"), sems("recv")
    r_tpz = Ring(NZ, z, zpeer, tpzi)
    r_tpg = Ring(NZ, z, zpeer, tpg)

    def send_token_b():
        low_in = dot(ah[...], actsf[...], NT)
        for k in range(2):
            parts = jnp.concatenate(pieces(low_in[k * RANK : (k + 1) * RANK], 3), axis=0)
            for yy in range(NY):
                t = dot(parts, gf[2 * yy + k])
                tbp[2 * yy + k] = t[0:RANK] + t[RANK : 2 * RANK] + t[2 * RANK :]
        tbi[q] = tbp[q]
        r_tb.start(lambda i: tbp.at[i])

    def send_tokens():
        r_ns.wait()
        low = []
        for lo in range(0, PAIR, TILE):
            rows = slice(lo, lo + TILE)
            halves = []
            for k in range(2):
                acc = None
                for yy in range(NY):
                    i = 2 * yy + k
                    s = (gf[i, rows, :].astype(F32) * ns[i, 1:2]).astype(BF16)
                    scaled[i, rows, :] = s
                    t = dot(s, bf[yy, k], NT)
                    acc = t if acc is None else acc + t
                halves.append(acc)
            low.append(jnp.concatenate(halves, axis=1))
        lowf = jnp.concatenate(low, axis=0)
        lowo[...] = lowf.astype(BF16)
        lowt = lowf.T.astype(BF16)
        for j in range(2):
            tpp[j] = dot(lowt, actsf[:, j * ROWS : (j + 1) * ROWS])
        copy(tpp.at[slot_of(1)], tpi, s_tpx, r_tpx, across_x).start()
        sent(tpi, s_tpx)

    def sum_tokens_x():
        arrived(tpi, r_tpx)
        tps[...] = (tpp[own_slot] + tpi[...]).reshape(NZ, 8, ROWS)
        tpzi[z] = tps[z]
        r_tpz.start(lambda i: tps.at[i])

    def sum_tokens_z():
        r_tpz.wait()
        tpg[z] = total(tpzi, NZ)
        r_tpg.start(lambda _: tpg.at[z])

    def sum_products_q():
        r_tb.wait()
        token_b = total(tbi, NQ)
        for g in range(NZ):
            ctp[g, 0:4] = across[4 * g : 4 * g + 4]
            ctp[g, 4:8] = token_b[4 * g : 4 * g + 4]
        cti[z] = ctp[z]
        r_ctz.start(lambda i: ctp.at[i])

    def sum_products_z():
        r_ctz.wait()
        ctx[x] = total(cti, NZ)
        r_ctx.start(lambda _: ctx.at[x])

    def sum_products_x():
        r_ctx.wait()
        ctz[z] = total(ctx, NX)
        r_ctg.start(lambda _: ctz.at[z])

    def column_sums(way, s):
        bx_wait(way, s)
        forward(origin(way, s))

    ring_b(1)
    ring_a(0, 1)
    cot_relay()
    ring_a(1, 1)
    ring_b(2)
    ring_a(0, 2)
    r_b.wait()
    cot_relay_last()
    ring_a(1, 2)
    ring_b(3)
    cot_wait()
    acts_wait()
    send_tokens()
    send_token_b()
    ring_a(0, 3)
    ring_a(1, 3)
    column_sums(0, 0)
    ring_b(4)
    column_sums(0, 1)
    column_sums(1, 1)
    ring_a(0, 4)
    column_sums(0, 2)
    column_sums(1, 2)
    ring_a(1, 4)
    column_sums(0, 3)
    column_sums(1, 3)
    sum_tokens_x()
    bx4_wait()
    forward(origin(0, 4))

    r_mox = Ring(NX, x, xpeer, mox)
    r_moz = Ring(NZ, z, zpeer, moz)
    r_moq = Ring(NQ, q, qpeer, moq)
    extra = []
    for i in range(NQ):
        extra.append(jnp.sum(tbp[i] * bf[i // 2, i % 2].astype(F32), axis=0, keepdims=True))
    mox[x] = momt[...] + jnp.concatenate(extra, axis=0)
    r_mox.start(lambda _: mox.at[x])

    s_gx, r_gx = sems("send"), sems("recv")
    l_gx = sems("local")

    def backward(j):
        cols = slice(j * ROWS, (j + 1) * ROWS)
        acc = dot(lowo[...], ah[:, cols])
        for zi in range(NZ):
            acc = acc + dot(scaled[zi], w[zi, j], NT)
        gxb[:, cols] = acc.astype(BF16)

    def gx_start(j):
        there = gx_out.at[:, shard(p, h, j)]
        part = pl.ds(j * ROWS, ROWS)
        for core_of, half_of, dev in ((p, 1 - h, partner), (1 - p, 1 - h, cross), (1 - p, h, core)):
            copy(gxb.at[tokens_of(core_of, half_of), part], there, s_gx, r_gx, dev).start()
        pltpu.make_async_copy(gxb.at[mine, part], there, lsem.at[l_gx]).start()

    backward(0)
    gx_start(0)
    sum_products_q()
    r_mox.wait()
    moz[z] = total(mox, NX)
    r_moz.start(lambda _: moz.at[z])
    backward(1)
    sum_tokens_z()
    sum_products_z()
    gx_start(1)
    r_moz.wait()
    moq[q] = total(moz, NZ)
    r_moq.start(lambda _: moq.at[q])
    r_moq.wait()
    moment = total(moq, NQ)
    norm_all = jnp.concatenate([ns[i, 0:1] for i in range(NQ)], axis=0)
    scal_all = jnp.concatenate([ns[i, 1:2] for i in range(NQ)], axis=0)
    grad_mag = moment / norm_all
    factor = scal_all * grad_mag / norm_all
    momt[...] = grad_mag

    for k in range(2):
        inner = None
        for yy in range(NY):
            i = 2 * yy + k
            two = jnp.concatenate(pieces(bf[yy, k].astype(F32) * factor[i : i + 1], 2), axis=0)
            wts[i] = two
            t = dot(two, bf[yy, k], NT)
            inner = t if inner is None else inner + t
        inr[k] = jnp.concatenate(pieces(inner[0:RANK] + inner[RANK:], 2), axis=0)

    s_ga, s_gac = sems("send"), sems("send")
    r_first, r_second, r_gac = sems("recv", NX), sems("recv", 3 * NX), sems("recv")

    def ga_block(k, a, b):
        dy, dx = (a, b) if k == 0 else (b, a)
        block = gaf.at[2 * lax.rem(y - dy + NY, NY) + p, lax.rem(x - dx + NX, NX)]
        return block.at[pl.ds(k * RANK, RANK), :]

    def ga_peer(k, axis, d):
        return ypeer(d) if k == axis else xpeer(d)

    def ga_core(here):
        copy(here, here, s_gac, r_gac, core).start()

    def ga_second(k, a):
        here = ga_block(k, a, 0)
        for turn in range(2):
            sem = r_second + 3 * a + turn
            copy(here, here, s_ga, sem, ga_peer(k, 1, 1 if turn == 0 else 3)).start()
        ga_core(here)

    def ga_start(k):
        here = ga_block(k, 0, 0)
        for d in (1, 3, 2):
            copy(here, here, s_ga, r_first + d, ga_peer(k, 0, d)).start()
        ga_second(k, 0)

    whole = gaf.at[0, 0]

    def ga_first(a):
        arrived(whole, r_first + a)
        for k in range(2):
            ga_second(k, a)

    def ga_forward(a):
        for turn in range(2):
            arrived(whole, r_second + 3 * a + turn)
            for k in range(2):
                here = ga_block(k, a, 1 if turn == 0 else 3)
                if (a in (0, 2)) == (turn == 0):
                    sem = r_second + 3 * a + 2
                    copy(here, here, s_ga, sem, ga_peer(k, 1, 1 if turn == 0 else 3)).start()
                ga_core(here)

    def ga_last(a):
        arrived(whole, r_second + 3 * a + 2)
        for k in range(2):
            ga_core(ga_block(k, a, 2))

    r_tpg.wait()
    tokens = tpg[...].reshape(2 * RANK, ROWS)
    span = pl.ds(pl.multiple_of(own_slot * ROWS, 128), ROWS)
    for k in range(2):
        acc = dot(inr[k], ah[k * RANK : (k + 1) * RANK, span])
        for yy in range(NY):
            acc = acc + dot(wts[2 * yy + k], w[2 * yy + k, own_slot], NT)
        rows = slice(k * RANK, (k + 1) * RANK)
        gaf[q, x, rows, :] = (tokens[rows] - (acc[0:RANK] + acc[RANK:])).astype(BF16)
        ga_start(k)

    sum_products_x()
    ga_first(1)
    ga_first(3)
    ga_forward(0)
    ga_first(2)
    ga_forward(1)
    ga_forward(3)
    ga_forward(2)
    r_ctg.wait()
    ctc[p] = ctz[...]
    s_ctc, r_ctc = sems("send"), sems("recv")
    copy(ctc.at[p], ctc.at[p], s_ctc, r_ctc, core).start()
    sent(ctc.at[p], s_ctc)
    for a in (0, 1, 3, 2):
        ga_last(a)
    arrived(ctc.at[1 - p], r_ctc)
    for k in range(2):
        i = 2 * y + k
        norm_k = ns[i, 0:1]
        scal_k = ns[i, 1:2]
        gm_k = momt[pl.ds(i, 1), :]
        gm_out[k : k + 1] = gm_k
        ratio = gm_k / norm_k
        for g in range(NZ):
            gb_out[k, 4 * g : 4 * g + 4] = scal_k * (ctc[k, g, 4:8] - ctc[k, g, 0:4] * ratio)

    arrived(gaf.at[pl.ds(0, NY)], r_gac)
    arrived(gxb.at[pl.ds(0, 3 * TOK), :], r_gx)
    sent(gxb.at[pl.ds(0, 3 * TOK), :], s_gx)
    pltpu.make_async_copy(gxb.at[mine, :], gxb.at[mine, :], lsem.at[l_gx]).wait()
    sent(gaf.at[pl.ds(0, 5), pl.ds(0, 3)], s_ga)
    sent(gaf.at[pl.ds(0, NY)], s_gac)
    assert counts == limits, counts
    for final in finals:
        final()


SENDS, RECVS, LOCALS = 27, 77, 11


def finish(gx, ga, gb, gm):
    def widen(gx_in, ga_in, gb_in, gm_in, gx_to, ga_to, gb_to, gm_to, full, gx_sem, ga_sem):
        pltpu.make_async_copy(gx_in, gx_to, gx_sem).start()
        gb_to[...] = gb_in[...]
        gm_to[...] = gm_in[...]
        for i in range(NQ):
            for xx in range(NX):
                for k in range(2):
                    block = ga_in[i, xx, k * RANK : (k + 1) * RANK, :]
                    full[i, k, :, xx * ROWS : (xx + 1) * ROWS] = block.astype(F32)
            pltpu.make_async_copy(full.at[i], ga_to.at[:, :, pl.ds(i * HALF, HALF)], ga_sem).start()
        pltpu.make_async_copy(full, full, ga_sem).wait()
        pltpu.make_async_copy(gx_in, gx_in, gx_sem).wait()

    vm = pl.BlockSpec(memory_space=pltpu.VMEM)
    hbm = pl.BlockSpec(memory_space=pl.ANY)
    return pl.pallas_call(
        widen,
        out_shape=(
            jax.ShapeDtypeStruct(gx.shape, BF16),
            jax.ShapeDtypeStruct((2, RANK, NQ * HALF), F32),
            jax.ShapeDtypeStruct(gb.shape, F32),
            jax.ShapeDtypeStruct(gm.shape, F32),
        ),
        in_specs=[vm, vm, vm, vm],
        out_specs=(hbm, hbm, vm, vm),
        scratch_shapes=[
            pltpu.VMEM((NQ, 2, RANK, HALF), F32),
            pltpu.SemaphoreType.DMA,
            pltpu.SemaphoreType.DMA,
        ],
        compiler_params=pltpu.CompilerParams(vmem_limit_bytes=16 * 2**20),
    )(gx, ga, gb, gm)


def on_device(acts, cot, base, adapter_a, adapter_b, magnitude):
    at = jnp.swapaxes(adapter_a, 1, 2)
    vm = pl.BlockSpec(memory_space=pltpu.VMEM)
    hbm = pl.BlockSpec(memory_space=pl.ANY)
    scratch = [
        ((NZ, 2, ROWS, COLS), BF16),
        ((PAIR, WORK), BF16),
        ((NQ, PAIR, COLS), BF16),
        ((NQ, PAIR, COLS), BF16),
        ((NY, 2, RANK, COLS), BF16),
        ((2 * RANK, WORK), BF16),
        ((RANK, ROWS), BF16),
        ((ROWS, COLS), BF16),
        ((NX, 8, COLS), F32),
        ((NZ, 8, COLS), F32),
        ((NQ, 8, COLS), F32),
        ((NQ, RANK, COLS), F32),
        ((NQ, RANK, COLS), F32),
        ((NZ, 8, COLS), F32),
        ((NZ, 8, COLS), F32),
        ((NX, 8, COLS), F32),
        ((NZ, 8, COLS), F32),
        ((2, NZ, 8, COLS), F32),
        ((2, 2 * RANK, ROWS), F32),
        ((2 * RANK, ROWS), F32),
        ((NZ, 8, ROWS), F32),
        ((NZ, 8, ROWS), F32),
        ((NZ, 8, ROWS), F32),
        ((NX, 8, COLS), F32),
        ((NZ, 8, COLS), F32),
        ((NQ, 8, COLS), F32),
        ((PAIR, WORK), BF16),
        ((PAIR, 2 * RANK), BF16),
        ((NQ, COLS), F32),
        ((NQ, 2 * RANK, COLS), BF16),
        ((2, 2 * RANK, RANK), BF16),
    ]
    gx, ga, gb, gm = pl.pallas_call(
        kernel,
        out_shape=(
            pltpu.VMEM((TOK, FEAT), BF16),
            pltpu.VMEM((NQ, NX, 2 * RANK, ROWS), BF16),
            pltpu.VMEM((2, RANK, COLS), F32),
            pltpu.VMEM((2, COLS), F32),
        ),
        in_specs=[hbm, hbm, hbm, hbm, vm, vm],
        out_specs=(vm, vm, vm, vm),
        scratch_shapes=[pltpu.VMEM(shape, dtype) for shape, dtype in scratch]
        + [pltpu.SemaphoreType.DMA((n,)) for n in (SENDS, RECVS, LOCALS)],
        compiler_params=pltpu.CompilerParams(
            collective_id=0, has_side_effects=True, vmem_limit_bytes=58 * 2**20
        ),
        cost_estimate=pl.CostEstimate(flops=5 * 10**9, bytes_accessed=8 * 10**6, transcendentals=0),
    )(acts, cot, base, at, adapter_b, magnitude)
    gx, ga, gb, gm = finish(gx, ga, gb, gm)
    return gx, jnp.swapaxes(ga, 1, 2), gb, gm


def solution(mesh):
    in_specs = (
        P(("dp", "fsdp"), "col"),
        P(None, ("dp", "fsdp"), "col"),
        P(None, "fsdp", "col"),
        P(),
        P(None, None, "col"),
        P(None, "col"),
    )
    out_specs = (P(("dp", "fsdp"), "col"), P(), P(None, None, "col"), P(None, "col"))
    return jax.shard_map(
        on_device, mesh=mesh, in_specs=in_specs, out_specs=out_specs, check_vma=False
    )
```
